128 devices in a mesh: expert: 4 (over x), row: 16 (over z, y), col: 2 (over core).
Axes of the slice: x: 4, y: 4, z: 4, core: 2. Of those that a mesh axis runs over, the one named last changes fastest.
Arguments:
- tokens: bfloat16 [8192, 4096], P(('expert', 'row'), 'col'), may hold values from -6 to 6
- router: bfloat16 [4096, 4], P('col'), may hold values from -0.09375 to 0.09375
- up_weight: bfloat16 [4, 4096, 14336], P('expert', 'col', 'row'), may hold values from -0.09375 to 0.09375
- down_weight: bfloat16 [4, 14336, 4096], P('expert', 'row', 'col'), may hold values from -0.046875 to 0.046875
- choices: int32 [64, 4, 8], P(('expert', 'row')), may hold values from -1 to 127, as said below
Outputs:
- mixed: bfloat16 [8192, 4096], P(('expert', 'row'), 'col')
The draws below stay inside these ranges and needn't reach their ends.
Inputs may be any that keep to these rules, and one draw needn't show every extreme that they name: `choices`: entry [s, e] lists, as local rows of source block s's 128 tokens, the tokens that expert e chooses from that block, distinct and ascending, followed by -1 padding. Each expert chooses exactly 384 tokens in all; from one block it chooses at least 4 and at most 8, and for every expert some block fills all 8 slots.
All inputs are finite; a program needn't handle non-finite values.
Results may differ from the reference program's by a relative error of at most 0.02.
Values may be sent and summed in bfloat16 or wider, within the bound.
No kernel may reach another device: no remote copies, remote signals or barrier semaphores. Data moves between devices by JAX's collectives and lax.ppermute only.
A program may use at most 64 MiB of HBM per device.

```python
import jax
import jax.numpy as jnp
from jax import lax

D = 4096
FF = 14336
TOK_DEV = 128
PER_SRC = 6
SPREAD = 2
SLOT = 8
EXPERTS = 4
SOURCES = 64
CAP = 384
TOKENS = 8192


def draw_choices(key, part):
    key = jax.random.fold_in(key, 11)
    pair_key, pick_key = jax.random.split(key)

    def counts_for(count_key):
        order_key, shift_key = jax.random.split(count_key)
        order = jax.random.permutation(order_key, SOURCES)
        shift = jax.random.randint(shift_key, (SOURCES // 2,), 0, SPREAD + 1)
        shift = shift.at[0].set(SPREAD)
        counts = jnp.zeros((SOURCES,), jnp.int32)
        counts = counts.at[order[0::2]].set(PER_SRC + shift)
        counts = counts.at[order[1::2]].set(PER_SRC - shift)
        return counts
    counts = jax.vmap(counts_for)(jax.random.split(pair_key, EXPERTS))
    pick_keys = jax.random.split(pick_key, SOURCES * EXPERTS)

    def pick(one_key, count):
        chosen = jax.random.permutation(one_key, TOK_DEV)[:SLOT]
        values = jnp.where(jnp.arange(SLOT) < count, chosen, TOK_DEV)
        values = jnp.sort(values)
        return jnp.where(values < TOK_DEV, values, -1)
    flat_counts = jnp.transpose(counts).reshape(SOURCES * EXPERTS)
    picked = jax.vmap(pick)(pick_keys, flat_counts)
    return picked.reshape(SOURCES, EXPERTS, SLOT).astype(jnp.int32)


def shard_levels(rng, dims, pieces, smallest, high):
    level, own = 1.0, jax.random.fold_in(rng, 6)
    for position, blocks in pieces:
        steps = jnp.exp(jax.random.uniform(jax.random.fold_in(own, position), (blocks,), jnp.float32, smallest / len(pieces), high / len(pieces)))
        level = level * jnp.repeat(steps, dims[position] // blocks).reshape([-1 if axis == position else 1 for axis in range(len(dims))])
    return level


def centred(own_key, dims, deviation, bound, pieces=(), kind=jnp.bfloat16):
    gain = shard_levels(own_key, dims, pieces, -0.22, 0.18) if pieces else 1.0
    array = jax.random.normal(own_key, dims, jnp.float32) * deviation * gain
    return jnp.minimum(jnp.maximum(array, -bound), bound).astype(kind)


def setup_inputs(seed: int = 0) -> dict:
    arg_keys = jax.random.split(jax.random.key(seed), 6)
    tokens = centred(arg_keys[0], (TOKENS, D), 1.0, 6.0, ((0, 64), (1, 2)))
    router = centred(arg_keys[1], (D, EXPERTS), D ** -0.5, 0.09375, ((0, 2),))
    up_weight = centred(arg_keys[2], (EXPERTS, D, FF), D ** -0.5, 0.09375, ((0, 4), (1, 2), (2, 16)))
    down_weight = centred(arg_keys[3], (EXPERTS, FF, D), FF ** -0.5, 0.046875, ((0, 4), (1, 16), (2, 2)))
    choices = draw_choices(jax.random.fold_in(arg_keys[5], 71), 0)
    return dict(tokens=tokens, router=router, up_weight=up_weight, down_weight=down_weight, choices=choices)


def expert_lists(choices):
    live = choices >= 0
    source = jnp.arange(SOURCES, dtype=jnp.int32)[:, None, None]
    token_index = jnp.where(live, source * TOK_DEV + choices, TOKENS).astype(jnp.int32)
    flat_live = jnp.transpose(live, (1, 0, 2)).reshape(EXPERTS, SOURCES * SLOT)
    flat_index = jnp.transpose(token_index, (1, 0, 2)).reshape(EXPERTS, SOURCES * SLOT)

    def place(live_row, index_row):
        where_to = jnp.where(live_row, jnp.cumsum(live_row.astype(jnp.int32)) - 1, CAP).astype(jnp.int32)
        filled = jnp.full((CAP + 1,), TOKENS, jnp.int32).at[where_to].set(index_row)
        return filled[:CAP]

    return jax.vmap(place)(flat_live, flat_index)


def reference(tokens, router, up_weight, down_weight, choices):
    gates = jax.nn.sigmoid(jnp.dot(tokens, router, preferred_element_type=jnp.float32))
    lists = expert_lists(choices)

    def one_expert(expert, total):
        picked = lists[expert]
        rows = tokens[picked]
        up_part = jnp.dot(rows, up_weight[expert], preferred_element_type=jnp.float32)
        hidden = jax.nn.gelu(up_part, approximate=True).astype(jnp.bfloat16)
        result = jnp.dot(hidden, down_weight[expert], preferred_element_type=jnp.float32).astype(jnp.bfloat16)
        weight = gates[picked, expert]
        return total.at[picked].add(weight[:, None] * result.astype(jnp.float32))

    total = lax.fori_loop(0, EXPERTS, one_expert, jnp.zeros((TOKENS, D), jnp.float32))
    return total.astype(jnp.bfloat16)
```

```python
import jax
import jax.numpy as jnp
from jax import lax
from jax.sharding import PartitionSpec as P

CHUNKS = 1


def on_device(tokens, router, up_weight, down_weight, choices):
    n_expert = lax.axis_size("expert")
    n_row = lax.axis_size("row")
    sources = n_expert * n_row
    slots = choices.shape[2]
    width = tokens.shape[1]
    local_tokens = tokens.shape[0]
    swap = [(0, 1), (1, 0)]
    local_ids = choices[0]
    token_rows = jnp.arange(local_tokens, dtype=jnp.int32)
    up_local = up_weight[0]
    down_local = down_weight[0]
    part = slots // CHUNKS
    merged = []
    for c in range(CHUNKS):
        ids = local_ids[:, c * part : (c + 1) * part]
        pick = (ids[:, :, None] == token_rows).astype(jnp.bfloat16)
        picked = jnp.dot(
            pick.reshape(n_expert * part, local_tokens), tokens, preferred_element_type=jnp.float32
        ).astype(jnp.bfloat16)
        spread = jnp.broadcast_to(
            picked.reshape(n_expert, 1, part, width), (n_expert, n_row, part, width)
        ).reshape(sources, part, width)
        rows = lax.all_to_all(spread, ("expert", "row"), split_axis=0, concat_axis=0, tiled=True)
        up_part = jnp.dot(
            rows.reshape(sources * part, width), up_local, preferred_element_type=jnp.float32
        )
        other = lax.ppermute(up_part.astype(jnp.bfloat16), "col", swap)
        hidden = jax.nn.gelu(up_part + other.astype(jnp.float32), approximate=True).astype(
            jnp.bfloat16
        )
        out = jnp.dot(hidden, down_local, preferred_element_type=jnp.float32).astype(jnp.bfloat16)
        arrived = lax.all_to_all(
            out.reshape(sources, part, width),
            ("expert", "row"),
            split_axis=0,
            concat_axis=0,
            tiled=True,
        )
        merged.append(
            jnp.sum(arrived.reshape(n_expert, n_row, part, width).astype(jnp.float32), axis=1)
        )
    logits = jnp.dot(tokens, router, preferred_element_type=jnp.float32)
    gates = jax.nn.sigmoid(logits + lax.ppermute(logits, "col", swap))
    y = jnp.concatenate(merged, axis=1)
    weights = (local_ids[None] == token_rows[:, None, None]).astype(jnp.float32) * gates[:, :, None]
    mixed = jnp.dot(
        weights.reshape(local_tokens, n_expert * slots),
        y.reshape(n_expert * slots, width),
        precision=lax.Precision.HIGHEST,
        preferred_element_type=jnp.float32,
    )
    return mixed.astype(jnp.bfloat16)


def solution(mesh):
    return jax.shard_map(
        on_device,
        mesh=mesh,
        in_specs=(
            P(("expert", "row"), "col"),
            P("col", None),
            P("expert", "col", "row"),
            P("expert", "row", "col"),
            P(("expert", "row"), None, None),
        ),
        out_specs=P(("expert", "row"), "col"),
        check_vma=False,
    )
```

```python
import functools

import jax
import jax.numpy as jnp
from jax import lax
from jax.experimental import pallas as pl
from jax.experimental.pallas import tpu as pltpu
from jax.sharding import PartitionSpec as P

SIDE = 4
QUARTERS = 4
PER_SRC = 6
EMPTY = 8.0
VMEM = 16 * 1024 * 1024


def neighbour_perms():
    moves = []
    for near, far in ((1, 0), (-1, 0), (0, 1), (0, -1)):
        pairs = []
        for z in range(SIDE):
            for y in range(SIDE):
                for core in range(2):
                    dy, dz = (near, far) if core == 0 else (far, near)
                    to = ((z + dz) % SIDE) * SIDE + (y + dy) % SIDE
                    pairs.append(((z * SIDE + y) * 2 + core, to * 2 + core))
        moves.append(pairs)
    return moves


def slot_row(choices):
    experts, slots = choices.shape
    lane = lax.broadcasted_iota(jnp.int32, (slots, experts * slots), 1)
    slot = lax.broadcasted_iota(jnp.int32, (slots, experts * slots), 0)
    tile = (lane % slots == slot).astype(jnp.float32)
    spread = jnp.dot(choices.astype(jnp.float32), tile, preferred_element_type=jnp.float32)
    lane = lax.broadcasted_iota(jnp.int32, spread.shape, 1)
    expert = lax.broadcasted_iota(jnp.int32, spread.shape, 0)
    row = jnp.sum(jnp.where(lane // slots == expert, spread, 0.0), axis=0, keepdims=True)
    return row.astype(jnp.int32)


def one_hot(ids, local_tokens):
    return lax.broadcasted_iota(jnp.int32, (local_tokens, ids.shape[1]), 0) == ids


def pick_kernel(core_ref, tokens_ref, choices_ref, out_ref):
    experts, slots = choices_ref.shape[1:]
    local_tokens, width = tokens_ref.shape
    quarter = width // QUARTERS
    ids = slot_row(choices_ref[0])
    hot = one_hot(ids, local_tokens).astype(jnp.bfloat16)
    first = (lax.broadcasted_iota(jnp.int32, (8, ids.shape[1]), 0) == 0) & (ids < 0)
    contract = (((0,), (0,)), ((), ()))
    mark = lax.dot_general(
        first.astype(jnp.bfloat16),
        jnp.full((8, 128), EMPTY, jnp.bfloat16),
        contract,
        preferred_element_type=jnp.float32,
    )
    core = core_ref[0]
    parts = []
    for q in range(QUARTERS):
        part = lax.dot_general(
            hot,
            tokens_ref[:, q * quarter : (q + 1) * quarter],
            contract,
            preferred_element_type=jnp.float32,
        )
        part = jnp.concatenate([part[:, :128] + mark, part[:, 128:]], axis=1)
        parts.append(part.reshape(experts, slots, quarter).astype(jnp.bfloat16))
    for a in range(SIDE):
        for b in range(SIDE):
            k0, k1 = (b + 2 * a) % QUARTERS, (a + 2 * b) % QUARTERS
            value = parts[k0] if k0 == k1 else jnp.where(core == 0, parts[k0], parts[k1])
            for e in range(experts):
                out_ref[e * SIDE * SIDE + a * SIDE + b] = value[e]


def compact_kernel(x_ref, full_ref, left_ref, right_ref, where_ref):
    rows, quarter = x_ref.shape
    capacity = full_ref.shape[0]
    live = (x_ref[:, :128].astype(jnp.float32) < EMPTY - 1.0).astype(jnp.bfloat16)
    i = lax.broadcasted_iota(jnp.int32, (rows, rows), 0)
    j = lax.broadcasted_iota(jnp.int32, (rows, rows), 1)
    contract = (((0,), (0,)), ((), ()))
    upto = lax.dot_general(
        live, (i <= j).astype(jnp.bfloat16), contract, preferred_element_type=jnp.float32
    )[:8]
    before = jnp.where(j[:8] == 0, 0.0, pltpu.roll(upto, 1, 1))
    position = jnp.where(upto > before, before, -1.0).astype(jnp.int32)[:1]
    where = (lax.broadcasted_iota(jnp.int32, (capacity, rows), 0) == position).astype(jnp.bfloat16)
    where_ref[...] = where
    full = jnp.dot(where, x_ref[...], preferred_element_type=jnp.float32).astype(jnp.bfloat16)
    full_ref[...] = full
    left_ref[...] = full[:, : quarter // 2]
    right_ref[...] = full[:, quarter // 2 :]


def first_up_kernel(mine_ref, rows_ref, up_ref, out_ref):
    quarter = rows_ref.shape[1]
    start = pl.multiple_of(mine_ref[0] * quarter, quarter)
    out_ref[...] = jnp.dot(
        rows_ref[...], up_ref[pl.ds(start, quarter), :], preferred_element_type=jnp.float32
    )


def next_up_kernel(step, mine_ref, sum_ref, rows_ref, up_ref, out_ref):
    quarter = rows_ref.shape[1]
    start = pl.multiple_of((mine_ref[0] + step) % QUARTERS * quarter, quarter)
    out_ref[...] = sum_ref[...] + jnp.dot(
        rows_ref[...], up_ref[pl.ds(start, quarter), :], preferred_element_type=jnp.float32
    )


def far_up_kernel(mine_ref, sum_ref, left_ref, right_ref, up_ref, out_ref, send_ref):
    half = left_ref.shape[1]
    total = sum_ref[...]
    for index, rows_ref in enumerate((left_ref, right_ref)):
        start = (mine_ref[0] + 2) % QUARTERS * 2 * half + index * half
        total += jnp.dot(
            rows_ref[...],
            up_ref[pl.ds(pl.multiple_of(start, half), half), :],
            preferred_element_type=jnp.float32,
        )
    out_ref[...] = total
    send_ref[...] = total.astype(jnp.bfloat16)


def down_kernel(mine_ref, sum_ref, other_ref, down_ref, hidden_ref, near_ref, next_ref, left_ref, right_ref):
    rows = hidden_ref.shape[0]
    quarter, half = near_ref.shape[1], left_ref.shape[1]
    block = rows // 3
    for i in range(3):
        at = slice(i * block, (i + 1) * block)
        value = sum_ref[at, :] + other_ref[at, :].astype(jnp.float32)
        hidden = jax.nn.gelu(value, approximate=True).astype(jnp.bfloat16)
        hidden_ref[at, :] = hidden
        for out_ref, step, offset, size in (
            (near_ref, 1, 0, quarter),
            (next_ref, 3, 0, quarter),
            (left_ref, 2, 0, half),
            (right_ref, 2, half, half),
        ):
            start = (mine_ref[0] + step) % QUARTERS * quarter + offset
            out_ref[at, :] = jnp.dot(
                hidden,
                down_ref[:, pl.ds(pl.multiple_of(start, half), size)],
                preferred_element_type=jnp.float32,
            ).astype(jnp.bfloat16)


def own_down_kernel(
    mine_ref, hidden_ref, down_ref, where_ref, tokens_ref, router_ref, out_ref, turned_ref, logits_ref
):
    quarter = out_ref.shape[1]
    start = pl.multiple_of(mine_ref[0] * quarter, quarter)
    out_ref[...] = jnp.dot(
        hidden_ref[...], down_ref[:, pl.ds(start, quarter)], preferred_element_type=jnp.float32
    )
    turned_ref[...] = where_ref[...].astype(jnp.float32).T.astype(jnp.bfloat16)
    logits_ref[...] = lax.dot_general(
        tokens_ref[...], router_ref[...], (((1,), (1,)), ((), ())), preferred_element_type=jnp.float32
    )


def return_kernel(own_ref, near_ref, next_ref, left_ref, right_ref, turned_ref, out_ref):
    far = jnp.concatenate([left_ref[...], right_ref[...]], axis=1)
    total = own_ref[...] + near_ref[...].astype(jnp.float32) + next_ref[...].astype(jnp.float32)
    total = (total + far.astype(jnp.float32)).astype(jnp.bfloat16)
    out_ref[...] = jnp.dot(turned_ref[...], total, preferred_element_type=jnp.float32).astype(
        jnp.bfloat16
    )


def mix_kernel(core_ref, arrived_ref, choices_ref, logits_ref, other_ref, out_hbm, out_ref, sems):
    experts, slots = choices_ref.shape[1:]
    local_tokens, width = out_ref.shape
    quarter = width // QUARTERS
    ids = slot_row(choices_ref[0])
    gates = jax.nn.sigmoid(logits_ref[...] + other_ref[...])
    lane = lax.broadcasted_iota(jnp.int32, (local_tokens, experts * slots), 1)
    weights = jnp.zeros((local_tokens, experts * slots), jnp.float32)
    for e in range(experts):
        weights = jnp.where(lane // slots == e, gates[:, e : e + 1], weights)
    weights = jnp.where(one_hot(ids, local_tokens), weights, 0.0)
    high = weights.astype(jnp.bfloat16)
    low = (weights - high.astype(jnp.float32)).astype(jnp.bfloat16)
    core = core_ref[0]
    stores = []
    for q in range(QUARTERS):
        total = []
        for e in range(experts):
            part = jnp.zeros((slots, quarter), jnp.float32)
            for a in range(SIDE):
                b = (q - 2 * a) % QUARTERS
                at = jnp.where(core == 0, a * SIDE + b, b * SIDE + a)
                part += arrived_ref[e * SIDE * SIDE + at].astype(jnp.float32)
            total.append(part)
        total = jnp.concatenate(total, axis=0).astype(jnp.bfloat16)
        mixed = jnp.dot(high, total, preferred_element_type=jnp.float32)
        mixed += jnp.dot(low, total, preferred_element_type=jnp.float32)
        at = pl.ds(q * quarter, quarter)
        out_ref[:, at] = mixed.astype(jnp.bfloat16)
        stores.append(pltpu.make_async_copy(out_ref.at[:, at], out_hbm.at[:, at], sems.at[q]))
        stores[-1].start()
    for store in stores:
        store.wait()


def call(kernel, scalars, arrays, outs, scratch=(), space=pltpu.VMEM):
    vmem = lambda: pl.BlockSpec(memory_space=pltpu.VMEM)
    return pl.pallas_call(
        kernel,
        out_shape=outs,
        in_specs=[pl.BlockSpec(memory_space=pltpu.SMEM) for _ in scalars]
        + [vmem() for _ in arrays],
        out_specs=jax.tree.map(lambda _: pl.BlockSpec(memory_space=space), outs),
        scratch_shapes=list(scratch),
        compiler_params=pltpu.CompilerParams(vmem_limit_bytes=VMEM),
    )(*scalars, *arrays)


def on_device(tokens, router, up_weight, down_weight, choices):
    n_expert = lax.axis_size("expert")
    n_row = lax.axis_size("row")
    sources = n_expert * n_row
    slots = choices.shape[2]
    local_tokens, width = tokens.shape
    quarter = width // QUARTERS
    half = quarter // 2
    capacity = PER_SRC * sources
    swap = [(0, 1), (1, 0)]
    moves = neighbour_perms()
    core = lax.axis_index("col")
    row = lax.axis_index("row")
    z, y = row // SIDE, row % SIDE
    mine = jnp.where(core == 0, y + 2 * z, z + 2 * y) % QUARTERS
    core_at = core.astype(jnp.int32).reshape(1)
    up_local = up_weight[0]
    down_local = down_weight[0]

    mine_at = mine.astype(jnp.int32).reshape(1)
    hidden_units = up_local.shape[1]

    def shape(*dims, dtype=jnp.bfloat16):
        return jax.ShapeDtypeStruct(dims, dtype)

    def move(array, which):
        return lax.ppermute(array, ("row", "col"), moves[which])

    spread = call(pick_kernel, [core_at], [tokens, choices], shape(sources, slots, quarter))
    own = lax.all_to_all(spread, ("expert", "row"), split_axis=0, concat_axis=0, tiled=True)
    full, left, right, where = call(
        compact_kernel,
        [],
        [own.reshape(sources * slots, quarter)],
        (
            shape(capacity, quarter),
            shape(capacity, half),
            shape(capacity, half),
            shape(capacity, sources * slots),
        ),
    )
    near, following, left, right = move(full, 0), move(full, 1), move(left, 2), move(right, 3)

    sums = shape(capacity, hidden_units, dtype=jnp.float32)
    up_part = call(first_up_kernel, [mine_at], [full, up_local], sums)
    for piece, step in ((near, 3), (following, 1)):
        up_part = call(
            functools.partial(next_up_kernel, step), [mine_at], [up_part, piece, up_local], sums
        )
    up_part, send = call(
        far_up_kernel,
        [mine_at],
        [up_part, left, right, up_local],
        (sums, shape(capacity, hidden_units)),
    )
    other = lax.ppermute(send, "col", swap)

    hidden, near, following, left, right = call(
        down_kernel,
        [mine_at],
        [up_part, other, down_local],
        (
            shape(capacity, hidden_units),
            shape(capacity, quarter),
            shape(capacity, quarter),
            shape(capacity, half),
            shape(capacity, half),
        ),
    )
    near, following, left, right = move(near, 0), move(following, 1), move(left, 2), move(right, 3)
    own, turned, logits = call(
        own_down_kernel,
        [mine_at],
        [hidden, down_local, where, tokens, router.T],
        (
            shape(capacity, quarter, dtype=jnp.float32),
            shape(sources * slots, capacity),
            shape(local_tokens, n_expert, dtype=jnp.float32),
        ),
    )
    other_logits = lax.ppermute(logits, "col", swap)
    out = call(
        return_kernel,
        [],
        [own, near, following, left, right, turned],
        shape(sources * slots, quarter),
    )
    out, logits, other_logits = lax.optimization_barrier((out, logits, other_logits))
    arrived = lax.all_to_all(
        out.reshape(sources, slots, quarter), ("expert", "row"), split_axis=0, concat_axis=0, tiled=True
    )
    return call(
        mix_kernel,
        [core_at],
        [arrived, choices, logits, other_logits],
        shape(local_tokens, width),
        scratch=[pltpu.VMEM(tokens.shape, jnp.bfloat16), pltpu.SemaphoreType.DMA((QUARTERS,))],
        space=pl.ANY,
    )


def solution(mesh):
    return jax.shard_map(
        on_device,
        mesh=mesh,
        in_specs=(
            P(("expert", "row"), "col"),
            P("col", None),
            P("expert", "col", "row"),
            P("expert", "row", "col"),
            P(("expert", "row"), None, None),
        ),
        out_specs=P(("expert", "row"), "col"),
        check_vma=False,
    )
```

```python
import functools

import jax
import jax.numpy as jnp
from jax import lax
from jax.experimental import pallas as pl
from jax.experimental.pallas import tpu as pltpu
from jax.sharding import PartitionSpec as P

SIDE = 4
QUARTERS = 4
PER_SRC = 6
EMPTY = 8.0
VMEM = 16 * 1024 * 1024
A, B, LEFT, RIGHT = ("own", 1), ("own", 3), ("other", 1), ("other", 3)
CHANGE = {A: 1, B: 3, LEFT: 2, RIGHT: 2}
DISPATCH = ((B, LEFT, 0, 8), (A, A, 0, 8), (LEFT, B, 0, 8))
RETURN = DISPATCH


def pairs_of(move):
    pairs = []
    for z in range(SIDE):
        for y in range(SIDE):
            for core in range(2):
                axis, flip = move[core]
                along_y = (axis == "own") == (core == 0)
                to = (z * SIDE + (y ^ flip)) if along_y else ((z ^ flip) * SIDE + y)
                pairs.append(((z * SIDE + y) * 2 + core, to * 2 + core))
    return pairs


def class_of(mine_ref, core_ref, move):
    change = [CHANGE[kind] for kind in move[:2]]
    if change[0] == change[1]:
        return mine_ref[0] ^ change[0]
    return mine_ref[0] ^ jnp.where(core_ref[0] == 0, change[0], change[1])


def slot_row(choices):
    experts, slots = choices.shape
    lane = lax.broadcasted_iota(jnp.int32, (slots, experts * slots), 1)
    slot = lax.broadcasted_iota(jnp.int32, (slots, experts * slots), 0)
    tile = (lane % slots == slot).astype(jnp.float32)
    spread = jnp.dot(choices.astype(jnp.float32), tile, preferred_element_type=jnp.float32)
    lane = lax.broadcasted_iota(jnp.int32, spread.shape, 1)
    expert = lax.broadcasted_iota(jnp.int32, spread.shape, 0)
    row = jnp.sum(jnp.where(lane // slots == expert, spread, 0.0), axis=0, keepdims=True)
    return row.astype(jnp.int32)


def one_hot(ids, local_tokens):
    return lax.broadcasted_iota(jnp.int32, (local_tokens, ids.shape[1]), 0) == ids


def pick_kernel(core_ref, tokens_ref, choices_ref, out_ref):
    experts, slots = choices_ref.shape
    local_tokens, width = tokens_ref.shape
    quarter = width // QUARTERS
    ids = slot_row(choices_ref[...])
    hot = one_hot(ids, local_tokens).astype(jnp.bfloat16)
    first = (lax.broadcasted_iota(jnp.int32, (8, ids.shape[1]), 0) == 0) & (ids >= local_tokens)
    contract = (((0,), (0,)), ((), ()))
    mark = lax.dot_general(
        first.astype(jnp.bfloat16),
        jnp.full((8, 128), EMPTY, jnp.bfloat16),
        contract,
        preferred_element_type=jnp.float32,
    )
    core = core_ref[0]
    parts = []
    for q in range(QUARTERS):
        part = lax.dot_general(
            hot,
            tokens_ref[:, q * quarter : (q + 1) * quarter],
            contract,
            preferred_element_type=jnp.float32,
        )
        part = jnp.concatenate([part[:, :128] + mark, part[:, 128:]], axis=1)
        parts.append(part.reshape(experts, slots, quarter).astype(jnp.bfloat16))
    for a in range(SIDE):
        for b in range(SIDE):
            k0, k1 = (b + 2 * a) % QUARTERS, (a + 2 * b) % QUARTERS
            value = parts[k0] if k0 == k1 else jnp.where(core == 0, parts[k0], parts[k1])
            for e in range(experts):
                out_ref[e * SIDE * SIDE + a * SIDE + b] = value[e]


def compact_kernel(x_ref, full_ref, where_ref):
    rows = x_ref.shape[0]
    capacity = full_ref.shape[0]
    live = (x_ref[:, :128].astype(jnp.float32) < EMPTY - 1.0).astype(jnp.bfloat16)
    i = lax.broadcasted_iota(jnp.int32, (rows, rows), 0)
    j = lax.broadcasted_iota(jnp.int32, (rows, rows), 1)
    contract = (((0,), (0,)), ((), ()))
    upto = lax.dot_general(
        live, (i <= j).astype(jnp.bfloat16), contract, preferred_element_type=jnp.float32
    )[:8]
    before = jnp.where(j[:8] == 0, 0.0, pltpu.roll(upto, 1, 1))
    position = jnp.where(upto > before, before, -1.0).astype(jnp.int32)[:1]
    where = (lax.broadcasted_iota(jnp.int32, (capacity, rows), 0) == position).astype(jnp.bfloat16)
    where_ref[...] = where
    full = jnp.dot(where, x_ref[...], preferred_element_type=jnp.float32)
    full_ref[...] = full.astype(jnp.bfloat16)


def up_product(where, rows_ref, up_ref):
    quarter = rows_ref.shape[1]
    start = pl.multiple_of(where * quarter, quarter)
    return jnp.dot(
        rows_ref[...], up_ref[pl.ds(start, quarter), :], preferred_element_type=jnp.float32
    )


def first_up_kernel(mine_ref, core_ref, rows_ref, up_ref, out_ref):
    out_ref[...] = up_product(mine_ref[0], rows_ref, up_ref)


def next_up_kernel(move, mine_ref, core_ref, sum_ref, rows_ref, up_ref, out_ref):
    at = class_of(mine_ref, core_ref, move)
    out_ref[...] = sum_ref[...] + up_product(at, rows_ref, up_ref)


def last_up_kernel(move, mine_ref, core_ref, sum_ref, rows_ref, up_ref, out_ref, send_ref):
    at = class_of(mine_ref, core_ref, move)
    total = sum_ref[...] + up_product(at, rows_ref, up_ref)
    out_ref[...] = total
    send_ref[...] = total.astype(jnp.bfloat16)


def down_kernel(mine_ref, core_ref, sum_ref, other_ref, down_ref, hidden_ref, *out_refs):
    rows = hidden_ref.shape[0]
    block = rows // 2
    for i in range(2):
        at = slice(i * block, (i + 1) * block)
        value = sum_ref[at, :] + other_ref[at, :].astype(jnp.float32)
        hidden = jax.nn.gelu(value, approximate=True).astype(jnp.bfloat16)
        hidden_ref[at, :] = hidden
        for move, out_ref in zip(RETURN, out_refs):
            first, last = move[2:]
            eighth = out_ref.shape[1] // (last - first)
            start = (class_of(mine_ref, core_ref, move) * 8 + first) * eighth
            columns = pl.ds(pl.multiple_of(start, 2 * eighth), out_ref.shape[1])
            out_ref[at, :] = jnp.dot(
                hidden, down_ref[:, columns], preferred_element_type=jnp.float32
            ).astype(jnp.bfloat16)


def own_down_kernel(
    mine_ref, hidden_ref, down_ref, where_ref, tokens_ref, router_ref, out_ref, turned_ref, logits_ref
):
    quarter = out_ref.shape[1]
    start = pl.multiple_of(mine_ref[0] * quarter, quarter)
    out_ref[...] = jnp.dot(
        hidden_ref[...], down_ref[:, pl.ds(start, quarter)], preferred_element_type=jnp.float32
    )
    turned_ref[...] = where_ref[...].astype(jnp.float32).T.astype(jnp.bfloat16)
    logits_ref[...] = lax.dot_general(
        tokens_ref[...], router_ref[...], (((1,), (1,)), ((), ())), preferred_element_type=jnp.float32
    )


def return_kernel(own_ref, *refs):
    *piece_refs, turned_ref, out_ref = refs
    half = out_ref.shape[1] // 2
    for i in range(2):
        at = slice(i * half, (i + 1) * half)
        total = own_ref[:, at]
        for (_, _, first, last), piece_ref in zip(RETURN, piece_refs):
            if last - first == 8:
                total += piece_ref[:, at].astype(jnp.float32)
            elif first == 4 * i:
                total += piece_ref[...].astype(jnp.float32)
        out_ref[:, at] = jnp.dot(
            turned_ref[...], total.astype(jnp.bfloat16), preferred_element_type=jnp.float32
        ).astype(jnp.bfloat16)


def weight_kernel(choices_ref, logits_ref, other_ref, high_ref, low_ref):
    experts, slots = choices_ref.shape
    local_tokens = logits_ref.shape[0]
    ids = slot_row(choices_ref[...])
    gates = jax.nn.sigmoid(logits_ref[...] + other_ref[...])
    lane = lax.broadcasted_iota(jnp.int32, (local_tokens, experts * slots), 1)
    weights = jnp.zeros((local_tokens, experts * slots), jnp.float32)
    for e in range(experts):
        weights = jnp.where(lane // slots == e, gates[:, e : e + 1], weights)
    weights = jnp.where(one_hot(ids, local_tokens), weights, 0.0)
    high = weights.astype(jnp.bfloat16)
    high_ref[...] = high
    low_ref[...] = (weights - high.astype(jnp.float32)).astype(jnp.bfloat16)


def mix_kernel(core_ref, arrived_ref, high_ref, low_ref, out_hbm, out_ref, sems):
    slots, quarter = arrived_ref.shape[1:]
    experts = arrived_ref.shape[0] // (SIDE * SIDE)
    high, low = high_ref[...], low_ref[...]
    core = core_ref[0]
    stores = []
    for q in range(QUARTERS):
        total = []
        for e in range(experts):
            part = jnp.zeros((slots, quarter), jnp.float32)
            for a in range(SIDE):
                b = (q - 2 * a) % QUARTERS
                at = jnp.where(core == 0, a * SIDE + b, b * SIDE + a)
                part += arrived_ref[e * SIDE * SIDE + at].astype(jnp.float32)
            total.append(part)
        total = jnp.concatenate(total, axis=0).astype(jnp.bfloat16)
        mixed = jnp.dot(high, total, preferred_element_type=jnp.float32)
        mixed += jnp.dot(low, total, preferred_element_type=jnp.float32)
        at = pl.ds(q * quarter, quarter)
        out_ref[:, at] = mixed.astype(jnp.bfloat16)
        stores.append(pltpu.make_async_copy(out_ref.at[:, at], out_hbm.at[:, at], sems.at[q]))
        stores[-1].start()
    for store in stores:
        store.wait()


def call(kernel, scalars, arrays, outs, scratch=(), space=pltpu.VMEM):
    vmem = lambda: pl.BlockSpec(memory_space=pltpu.VMEM)
    return pl.pallas_call(
        kernel,
        out_shape=outs,
        in_specs=[pl.BlockSpec(memory_space=pltpu.SMEM) for _ in scalars]
        + [vmem() for _ in arrays],
        out_specs=jax.tree.map(lambda _: pl.BlockSpec(memory_space=space), outs),
        scratch_shapes=list(scratch),
        compiler_params=pltpu.CompilerParams(vmem_limit_bytes=VMEM),
    )(*scalars, *arrays)


def on_device(tokens, router, up_weight, down_weight, choices):
    n_expert = lax.axis_size("expert")
    n_row = lax.axis_size("row")
    sources = n_expert * n_row
    slots = choices.shape[2]
    local_tokens, width = tokens.shape
    quarter = width // QUARTERS
    capacity = PER_SRC * sources
    swap = [(0, 1), (1, 0)]
    core = lax.axis_index("col")
    row = lax.axis_index("row")
    z, y = row // SIDE, row % SIDE
    mine = jnp.where(core == 0, y + 2 * z, z + 2 * y) % QUARTERS
    core_at = core.astype(jnp.int32).reshape(1)
    up_local = up_weight[0]
    down_local = down_weight[0]

    mine_at = mine.astype(jnp.int32).reshape(1)
    place = [mine_at, core_at]
    hidden_units = up_local.shape[1]

    def shape(*dims, dtype=jnp.bfloat16):
        return jax.ShapeDtypeStruct(dims, dtype)

    def send(array, move):
        return lax.ppermute(array, ("row", "col"), pairs_of(move))

    ids = jnp.where(choices[0] >= 0, choices[0], local_tokens)
    spread = call(pick_kernel, [core_at], [tokens, ids], shape(sources, slots, quarter))
    own = lax.all_to_all(spread, ("expert", "row"), split_axis=0, concat_axis=0, tiled=True)
    full, where = call(
        compact_kernel,
        [],
        [own.reshape(sources * slots, quarter)],
        (shape(capacity, quarter), shape(capacity, sources * slots)),
    )
    pieces = [send(full, move) for move in DISPATCH]

    sums = shape(capacity, hidden_units, dtype=jnp.float32)
    up_part = call(first_up_kernel, place, [full, up_local], sums)
    for move, piece in zip(DISPATCH[:-1], pieces):
        kernel = functools.partial(next_up_kernel, move)
        up_part = call(kernel, place, [up_part, piece, up_local], sums)
    up_part, rounded = call(
        functools.partial(last_up_kernel, DISPATCH[-1]),
        place,
        [up_part, pieces[-1], up_local],
        (sums, shape(capacity, hidden_units)),
    )
    other = lax.ppermute(rounded, "col", swap)

    hidden, *pieces = call(
        down_kernel,
        place,
        [up_part, other, down_local],
        (shape(capacity, hidden_units),)
        + tuple(shape(capacity, quarter // 8 * (last - first)) for _, _, first, last in RETURN),
    )
    pieces = [send(piece, move) for piece, move in zip(pieces, RETURN)]
    own, turned, logits = call(
        own_down_kernel,
        [mine_at],
        [hidden, down_local, where, tokens, router.T],
        (
            shape(capacity, quarter, dtype=jnp.float32),
            shape(sources * slots, capacity),
            shape(local_tokens, n_expert, dtype=jnp.float32),
        ),
    )
    weights = shape(local_tokens, n_expert * slots)
    high, low = call(
        weight_kernel, [], [ids, logits, lax.ppermute(logits, "col", swap)], (weights, weights)
    )
    own, high, low = lax.optimization_barrier((own, high, low))
    out = call(
        return_kernel,
        [],
        [own, *pieces, turned],
        shape(sources * slots, quarter),
    )
    arrived = lax.all_to_all(
        out.reshape(sources, slots, quarter), ("expert", "row"), split_axis=0, concat_axis=0, tiled=True
    )
    return call(
        mix_kernel,
        [core_at],
        [arrived, high, low],
        shape(local_tokens, width),
        scratch=[pltpu.VMEM(tokens.shape, jnp.bfloat16), pltpu.SemaphoreType.DMA((QUARTERS,))],
        space=pl.ANY,
    )


def solution(mesh):
    return jax.shard_map(
        on_device,
        mesh=mesh,
        in_specs=(
            P(("expert", "row"), "col"),
            P("col", None),
            P("expert", "col", "row"),
            P("expert", "row", "col"),
            P(("expert", "row"), None, None),
        ),
        out_specs=P(("expert", "row"), "col"),
        check_vma=False,
    )
```

```python
import functools

import jax
import jax.numpy as jnp
from jax import lax
from jax.experimental import pallas as pl
from jax.experimental.pallas import tpu as pltpu
from jax.sharding import PartitionSpec as P

SIDE = 4
QUARTERS = 4
PER_SRC = 6
EMPTY = 8.0
VMEM = 16 * 1024 * 1024
A, B, LEFT, RIGHT = ("own", 1), ("own", 3), ("other", 1), ("other", 3)
CHANGE = {A: 1, B: 3, LEFT: 2, RIGHT: 2}
DISPATCH = ((B, LEFT, 0, 8), (A, A, 0, 8), (LEFT, B, 0, 8))
RETURN = DISPATCH


def pairs_of(move):
    pairs = []
    for z in range(SIDE):
        for y in range(SIDE):
            for core in range(2):
                axis, flip = move[core]
                along_y = (axis == "own") == (core == 0)
                to = (z * SIDE + (y ^ flip)) if along_y else ((z ^ flip) * SIDE + y)
                pairs.append(((z * SIDE + y) * 2 + core, to * 2 + core))
    return pairs


def class_of(mine_ref, core_ref, move):
    change = [CHANGE[kind] for kind in move[:2]]
    if change[0] == change[1]:
        return mine_ref[0] ^ change[0]
    return mine_ref[0] ^ jnp.where(core_ref[0] == 0, change[0], change[1])


def slot_row(choices):
    experts, slots = choices.shape
    lane = lax.broadcasted_iota(jnp.int32, (slots, experts * slots), 1)
    slot = lax.broadcasted_iota(jnp.int32, (slots, experts * slots), 0)
    tile = (lane % slots == slot).astype(jnp.float32)
    spread = jnp.dot(choices.astype(jnp.float32), tile, preferred_element_type=jnp.float32)
    lane = lax.broadcasted_iota(jnp.int32, spread.shape, 1)
    expert = lax.broadcasted_iota(jnp.int32, spread.shape, 0)
    row = jnp.sum(jnp.where(lane // slots == expert, spread, 0.0), axis=0, keepdims=True)
    return row.astype(jnp.int32)


def one_hot(ids, local_tokens):
    return lax.broadcasted_iota(jnp.int32, (local_tokens, ids.shape[1]), 0) == ids


def spread_kernel(core_ref, picked_ref, hot_ref, out_ref):
    slots, quarter = out_ref.shape[1:]
    experts = out_ref.shape[0] // (SIDE * SIDE)
    live = jnp.sum(hot_ref[...].astype(jnp.float32), axis=1, keepdims=True)
    mark = jnp.broadcast_to((1.0 - live) * EMPTY, (experts * slots, 128))
    core = core_ref[0]
    parts = []
    for q in range(QUARTERS):
        part = picked_ref[:, q * quarter : (q + 1) * quarter]
        part = jnp.concatenate([part[:, :128] + mark, part[:, 128:]], axis=1)
        parts.append(part.reshape(experts, slots, quarter).astype(jnp.bfloat16))
    for a in range(SIDE):
        for b in range(SIDE):
            k0, k1 = (b + 2 * a) % QUARTERS, (a + 2 * b) % QUARTERS
            value = parts[k0] if k0 == k1 else jnp.where(core == 0, parts[k0], parts[k1])
            for e in range(experts):
                out_ref[e * SIDE * SIDE + a * SIDE + b] = value[e]


def compact_kernel(x_ref, full_ref, where_ref):
    rows = x_ref.shape[0]
    capacity = full_ref.shape[0]
    live = (x_ref[:, :128].astype(jnp.float32) < EMPTY - 1.0).astype(jnp.bfloat16)
    i = lax.broadcasted_iota(jnp.int32, (rows, rows), 0)
    j = lax.broadcasted_iota(jnp.int32, (rows, rows), 1)
    contract = (((0,), (0,)), ((), ()))
    upto = lax.dot_general(
        live, (i <= j).astype(jnp.bfloat16), contract, preferred_element_type=jnp.float32
    )[:8]
    before = jnp.where(j[:8] == 0, 0.0, pltpu.roll(upto, 1, 1))
    position = jnp.where(upto > before, before, -1.0).astype(jnp.int32)[:1]
    where = (lax.broadcasted_iota(jnp.int32, (capacity, rows), 0) == position).astype(jnp.bfloat16)
    where_ref[...] = where
    full = jnp.dot(where, x_ref[...], preferred_element_type=jnp.float32)
    full_ref[...] = full.astype(jnp.bfloat16)


def up_product(where, rows_ref, up_ref):
    quarter = rows_ref.shape[1]
    start = pl.multiple_of(where * quarter, quarter)
    return jnp.dot(
        rows_ref[...], up_ref[pl.ds(start, quarter), :], preferred_element_type=jnp.float32
    )


def first_up_kernel(mine_ref, core_ref, rows_ref, up_ref, out_ref):
    out_ref[...] = up_product(mine_ref[0], rows_ref, up_ref)


def next_up_kernel(move, mine_ref, core_ref, sum_ref, rows_ref, up_ref, out_ref):
    at = class_of(mine_ref, core_ref, move)
    out_ref[...] = sum_ref[...] + up_product(at, rows_ref, up_ref)


def last_up_kernel(move, mine_ref, core_ref, sum_ref, rows_ref, up_ref, out_ref, send_ref):
    at = class_of(mine_ref, core_ref, move)
    total = sum_ref[...] + up_product(at, rows_ref, up_ref)
    out_ref[...] = total
    send_ref[...] = total.astype(jnp.bfloat16)


def down_kernel(mine_ref, core_ref, sum_ref, other_ref, down_ref, hidden_ref, *out_refs):
    rows = hidden_ref.shape[0]
    block = rows // 2
    for i in range(2):
        at = slice(i * block, (i + 1) * block)
        value = sum_ref[at, :] + other_ref[at, :].astype(jnp.float32)
        hidden = jax.nn.gelu(value, approximate=True).astype(jnp.bfloat16)
        hidden_ref[at, :] = hidden
        for move, out_ref in zip(RETURN, out_refs):
            first, last = move[2:]
            eighth = out_ref.shape[1] // (last - first)
            start = (class_of(mine_ref, core_ref, move) * 8 + first) * eighth
            columns = pl.ds(pl.multiple_of(start, 2 * eighth), out_ref.shape[1])
            out_ref[at, :] = jnp.dot(
                hidden, down_ref[:, columns], preferred_element_type=jnp.float32
            ).astype(jnp.bfloat16)


def own_down_kernel(mine_ref, hidden_ref, down_ref, where_ref, out_ref, turned_ref):
    quarter = out_ref.shape[1]
    start = pl.multiple_of(mine_ref[0] * quarter, quarter)
    out_ref[...] = jnp.dot(
        hidden_ref[...], down_ref[:, pl.ds(start, quarter)], preferred_element_type=jnp.float32
    )
    turned_ref[...] = where_ref[...].astype(jnp.float32).T.astype(jnp.bfloat16)


def return_kernel(own_ref, *refs):
    *piece_refs, turned_ref, out_ref = refs
    half = out_ref.shape[1] // 2
    for i in range(2):
        at = slice(i * half, (i + 1) * half)
        total = own_ref[:, at]
        for (_, _, first, last), piece_ref in zip(RETURN, piece_refs):
            if last - first == 8:
                total += piece_ref[:, at].astype(jnp.float32)
            elif first == 4 * i:
                total += piece_ref[...].astype(jnp.float32)
        out_ref[:, at] = jnp.dot(
            turned_ref[...], total.astype(jnp.bfloat16), preferred_element_type=jnp.float32
        ).astype(jnp.bfloat16)


def weight_kernel(choices_ref, logits_ref, other_ref, high_ref, low_ref):
    experts, slots = choices_ref.shape[1:]
    local_tokens = logits_ref.shape[0]
    ids = slot_row(choices_ref[0])
    gates = jax.nn.sigmoid(logits_ref[...] + other_ref[...])
    lane = lax.broadcasted_iota(jnp.int32, (local_tokens, experts * slots), 1)
    weights = jnp.zeros((local_tokens, experts * slots), jnp.float32)
    for e in range(experts):
        weights = jnp.where(lane // slots == e, gates[:, e : e + 1], weights)
    weights = jnp.where(one_hot(ids, local_tokens), weights, 0.0)
    high = weights.astype(jnp.bfloat16)
    high_ref[...] = high
    low_ref[...] = (weights - high.astype(jnp.float32)).astype(jnp.bfloat16)


def mix_kernel(core_ref, arrived_ref, high_ref, low_ref, out_hbm, out_ref, sems):
    slots, quarter = arrived_ref.shape[1:]
    experts = arrived_ref.shape[0] // (SIDE * SIDE)
    high, low = high_ref[...], low_ref[...]
    core = core_ref[0]
    stores = []
    for q in range(QUARTERS):
        total = []
        for e in range(experts):
            part = jnp.zeros((slots, quarter), jnp.float32)
            for a in range(SIDE):
                b = (q - 2 * a) % QUARTERS
                at = jnp.where(core == 0, a * SIDE + b, b * SIDE + a)
                part += arrived_ref[e * SIDE * SIDE + at].astype(jnp.float32)
            total.append(part)
        total = jnp.concatenate(total, axis=0).astype(jnp.bfloat16)
        mixed = jnp.dot(high, total, preferred_element_type=jnp.float32)
        mixed += jnp.dot(low, total, preferred_element_type=jnp.float32)
        at = pl.ds(q * quarter, quarter)
        out_ref[:, at] = mixed.astype(jnp.bfloat16)
        stores.append(pltpu.make_async_copy(out_ref.at[:, at], out_hbm.at[:, at], sems.at[q]))
        stores[-1].start()
    for store in stores:
        store.wait()


def call(kernel, scalars, arrays, outs, scratch=(), space=pltpu.VMEM):
    vmem = lambda: pl.BlockSpec(memory_space=pltpu.VMEM)
    return pl.pallas_call(
        kernel,
        out_shape=outs,
        in_specs=[pl.BlockSpec(memory_space=pltpu.SMEM) for _ in scalars]
        + [vmem() for _ in arrays],
        out_specs=jax.tree.map(lambda _: pl.BlockSpec(memory_space=space), outs),
        scratch_shapes=list(scratch),
        compiler_params=pltpu.CompilerParams(vmem_limit_bytes=VMEM),
    )(*scalars, *arrays)


def on_device(tokens, router, up_weight, down_weight, choices):
    n_expert = lax.axis_size("expert")
    n_row = lax.axis_size("row")
    sources = n_expert * n_row
    slots = choices.shape[2]
    local_tokens, width = tokens.shape
    quarter = width // QUARTERS
    capacity = PER_SRC * sources
    swap = [(0, 1), (1, 0)]
    core = lax.axis_index("col")
    row = lax.axis_index("row")
    z, y = row // SIDE, row % SIDE
    mine = jnp.where(core == 0, y + 2 * z, z + 2 * y) % QUARTERS
    core_at = core.astype(jnp.int32).reshape(1)
    up_local = up_weight[0]
    down_local = down_weight[0]

    mine_at = mine.astype(jnp.int32).reshape(1)
    place = [mine_at, core_at]
    hidden_units = up_local.shape[1]

    def shape(*dims, dtype=jnp.bfloat16):
        return jax.ShapeDtypeStruct(dims, dtype)

    def send(array, move):
        return lax.ppermute(array, ("row", "col"), pairs_of(move))

    token_rows = jnp.arange(local_tokens, dtype=jnp.int32)
    hot = (choices[0][:, :, None] == token_rows).astype(jnp.bfloat16)
    hot = hot.reshape(n_expert * slots, local_tokens)
    picked = jnp.dot(hot, tokens, preferred_element_type=jnp.float32)
    spread = call(spread_kernel, [core_at], [picked, hot], shape(sources, slots, quarter))
    own = lax.all_to_all(spread, ("expert", "row"), split_axis=0, concat_axis=0, tiled=True)
    full, where = call(
        compact_kernel,
        [],
        [own.reshape(sources * slots, quarter)],
        (shape(capacity, quarter), shape(capacity, sources * slots)),
    )
    pieces = [send(full, move) for move in DISPATCH]

    sums = shape(capacity, hidden_units, dtype=jnp.float32)
    up_part = call(first_up_kernel, place, [full, up_local], sums)
    for move, piece in zip(DISPATCH[:-1], pieces):
        kernel = functools.partial(next_up_kernel, move)
        up_part = call(kernel, place, [up_part, piece, up_local], sums)
    up_part, rounded = call(
        functools.partial(last_up_kernel, DISPATCH[-1]),
        place,
        [up_part, pieces[-1], up_local],
        (sums, shape(capacity, hidden_units)),
    )
    other = lax.ppermute(rounded, "col", swap)

    hidden, *pieces = call(
        down_kernel,
        place,
        [up_part, other, down_local],
        (shape(capacity, hidden_units),)
        + tuple(shape(capacity, quarter // 8 * (last - first)) for _, _, first, last in RETURN),
    )
    pieces = [send(piece, move) for piece, move in zip(pieces, RETURN)]
    own, turned = call(
        own_down_kernel,
        [mine_at],
        [hidden, down_local, where],
        (
            shape(capacity, quarter, dtype=jnp.float32),
            shape(sources * slots, capacity),
        ),
    )
    late_router, own = lax.optimization_barrier((router, own))
    logits = jnp.dot(tokens, late_router, preferred_element_type=jnp.float32)
    weights = shape(local_tokens, n_expert * slots)
    high, low = call(
        weight_kernel, [], [choices, logits, lax.ppermute(logits, "col", swap)], (weights, weights)
    )
    own, high, low = lax.optimization_barrier((own, high, low))
    out = call(
        return_kernel,
        [],
        [own, *pieces, turned],
        shape(sources * slots, quarter),
    )
    arrived = lax.all_to_all(
        out.reshape(sources, slots, quarter), ("expert", "row"), split_axis=0, concat_axis=0, tiled=True
    )
    return call(
        mix_kernel,
        [core_at],
        [arrived, high, low],
        shape(local_tokens, width),
        scratch=[pltpu.VMEM(tokens.shape, jnp.bfloat16), pltpu.SemaphoreType.DMA((QUARTERS,))],
        space=pl.ANY,
    )


def solution(mesh):
    return jax.shard_map(
        on_device,
        mesh=mesh,
        in_specs=(
            P(("expert", "row"), "col"),
            P("col", None),
            P("expert", "col", "row"),
            P("expert", "row", "col"),
            P(("expert", "row"), None, None),
        ),
        out_specs=P(("expert", "row"), "col"),
        check_vma=False,
    )
```

```python
import functools

import jax
import jax.numpy as jnp
from jax import lax
from jax.experimental import pallas as pl
from jax.experimental.pallas import tpu as pltpu
from jax.sharding import PartitionSpec as P

SIDE = 4
QUARTERS = 4
BAND = 128
PER_SRC = 6
EMPTY = 8.0
VMEM = 16 * 1024 * 1024
A, B, LEFT, RIGHT = ("own", 1), ("own", 3), ("other", 1), ("other", 3)
CHANGE = {A: 1, B: 3, LEFT: 2, RIGHT: 2}
DISPATCH = ((B, LEFT, 0, 8), (A, A, 0, 8), (LEFT, B, 0, 8))
RETURN = DISPATCH


def pairs_of(move):
    pairs = []
    for z in range(SIDE):
        for y in range(SIDE):
            for core in range(2):
                axis, flip = move[core]
                along_y = (axis == "own") == (core == 0)
                to = (z * SIDE + (y ^ flip)) if along_y else ((z ^ flip) * SIDE + y)
                pairs.append(((z * SIDE + y) * 2 + core, to * 2 + core))
    return pairs


def class_of(mine_ref, core_ref, move):
    change = [CHANGE[kind] for kind in move[:2]]
    if change[0] == change[1]:
        return mine_ref[0] ^ change[0]
    return mine_ref[0] ^ jnp.where(core_ref[0] == 0, change[0], change[1])


def slot_row(choices):
    experts, slots = choices.shape
    lane = lax.broadcasted_iota(jnp.int32, (slots, experts * slots), 1)
    slot = lax.broadcasted_iota(jnp.int32, (slots, experts * slots), 0)
    tile = (lane % slots == slot).astype(jnp.float32)
    spread = jnp.dot(choices.astype(jnp.float32), tile, preferred_element_type=jnp.float32)
    lane = lax.broadcasted_iota(jnp.int32, spread.shape, 1)
    expert = lax.broadcasted_iota(jnp.int32, spread.shape, 0)
    row = jnp.sum(jnp.where(lane // slots == expert, spread, 0.0), axis=0, keepdims=True)
    return row.astype(jnp.int32)


def one_hot(ids, local_tokens):
    return lax.broadcasted_iota(jnp.int32, (local_tokens, ids.shape[1]), 0) == ids


def spread_kernel(core_ref, picked_ref, hot_ref, out_ref):
    slots, quarter = out_ref.shape[1:]
    experts = out_ref.shape[0] // (SIDE * SIDE)
    live = jnp.sum(hot_ref[...].astype(jnp.float32), axis=1, keepdims=True)
    mark = jnp.broadcast_to((1.0 - live) * EMPTY, (experts * slots, 128))
    core = core_ref[0]
    parts = []
    for q in range(QUARTERS):
        part = picked_ref[:, q * quarter : (q + 1) * quarter]
        part = jnp.concatenate([part[:, :128] + mark, part[:, 128:]], axis=1)
        parts.append(part.reshape(experts, slots, quarter).astype(jnp.bfloat16))
    for a in range(SIDE):
        for b in range(SIDE):
            k0, k1 = (b + 2 * a) % QUARTERS, (a + 2 * b) % QUARTERS
            value = parts[k0] if k0 == k1 else jnp.where(core == 0, parts[k0], parts[k1])
            for e in range(experts):
                out_ref[e * SIDE * SIDE + a * SIDE + b] = value[e]


def compact_kernel(x_ref, full_ref, where_ref):
    rows = x_ref.shape[0]
    capacity = full_ref.shape[0]
    live = (x_ref[:, :128].astype(jnp.float32) < EMPTY - 1.0).astype(jnp.bfloat16)
    i = lax.broadcasted_iota(jnp.int32, (rows, rows), 0)
    j = lax.broadcasted_iota(jnp.int32, (rows, rows), 1)
    contract = (((0,), (0,)), ((), ()))
    upto = lax.dot_general(
        live, (i <= j).astype(jnp.bfloat16), contract, preferred_element_type=jnp.float32
    )[:8]
    before = jnp.where(j[:8] == 0, 0.0, pltpu.roll(upto, 1, 1))
    position = jnp.where(upto > before, before, -1.0).astype(jnp.int32)[:1]
    for p in range(0, capacity, BAND):
        columns = slice(p, p + 2 * BAND)
        target = lax.broadcasted_iota(jnp.int32, (BAND, 2 * BAND), 0) + p
        where = (target == position[:, columns]).astype(jnp.bfloat16)
        where_ref[p : p + BAND, :] = where
        full_ref[p : p + BAND, :] = jnp.dot(
            where, x_ref[columns, :], preferred_element_type=jnp.float32
        ).astype(jnp.bfloat16)


def up_product(where, rows_ref, up_ref):
    quarter = rows_ref.shape[1]
    start = pl.multiple_of(where * quarter, quarter)
    return jnp.dot(
        rows_ref[...], up_ref[pl.ds(start, quarter), :], preferred_element_type=jnp.float32
    )


def first_up_kernel(mine_ref, core_ref, rows_ref, up_ref, out_ref):
    out_ref[...] = up_product(mine_ref[0], rows_ref, up_ref)


def next_up_kernel(move, mine_ref, core_ref, sum_ref, rows_ref, up_ref, out_ref):
    at = class_of(mine_ref, core_ref, move)
    out_ref[...] = sum_ref[...] + up_product(at, rows_ref, up_ref)


def last_up_kernel(move, mine_ref, core_ref, sum_ref, rows_ref, up_ref, out_ref, send_ref):
    at = class_of(mine_ref, core_ref, move)
    total = sum_ref[...] + up_product(at, rows_ref, up_ref)
    out_ref[...] = total
    send_ref[...] = total.astype(jnp.bfloat16)


def down_kernel(mine_ref, core_ref, sum_ref, other_ref, down_ref, hidden_ref, *out_refs):
    rows = hidden_ref.shape[0]
    block = rows // 2
    for i in range(2):
        at = slice(i * block, (i + 1) * block)
        value = sum_ref[at, :] + other_ref[at, :].astype(jnp.float32)
        hidden = jax.nn.gelu(value, approximate=True).astype(jnp.bfloat16)
        hidden_ref[at, :] = hidden
        for move, out_ref in zip(RETURN, out_refs):
            first, last = move[2:]
            eighth = out_ref.shape[1] // (last - first)
            start = (class_of(mine_ref, core_ref, move) * 8 + first) * eighth
            columns = pl.ds(pl.multiple_of(start, 2 * eighth), out_ref.shape[1])
            out_ref[at, :] = jnp.dot(
                hidden, down_ref[:, columns], preferred_element_type=jnp.float32
            ).astype(jnp.bfloat16)


def own_down_kernel(mine_ref, hidden_ref, down_ref, where_ref, out_ref, turned_ref):
    quarter = out_ref.shape[1]
    start = pl.multiple_of(mine_ref[0] * quarter, quarter)
    out_ref[...] = jnp.dot(
        hidden_ref[...], down_ref[:, pl.ds(start, quarter)], preferred_element_type=jnp.float32
    )
    for p in range(0, where_ref.shape[0], BAND):
        where = where_ref[p : p + BAND, :].astype(jnp.float32)
        turned_ref[p : p + BAND, BAND:] = where[:, :BAND].T.astype(jnp.bfloat16)
        turned_ref[p + BAND : p + 2 * BAND, :BAND] = where[:, BAND:].T.astype(jnp.bfloat16)


def return_kernel(own_ref, *refs):
    *piece_refs, turned_ref, out_ref = refs
    total = own_ref[...]
    for piece_ref in piece_refs:
        total += piece_ref[...].astype(jnp.float32)
    total = total.astype(jnp.bfloat16)
    for row in range(0, out_ref.shape[0], BAND):
        low, high = max(row - BAND, 0), min(row + BAND, total.shape[0])
        columns = slice(low - row + BAND, high - row + BAND)
        out_ref[row : row + BAND, :] = jnp.dot(
            turned_ref[row : row + BAND, columns], total[low:high], preferred_element_type=jnp.float32
        ).astype(jnp.bfloat16)


def weight_kernel(choices_ref, logits_ref, other_ref, out_ref):
    experts, slots = choices_ref.shape[1:]
    local_tokens = logits_ref.shape[0]
    ids = slot_row(choices_ref[0])
    gates = jax.nn.sigmoid(logits_ref[...] + other_ref[...])
    lane = lax.broadcasted_iota(jnp.int32, (local_tokens, experts * slots), 1)
    weights = jnp.zeros((local_tokens, experts * slots), jnp.float32)
    for e in range(experts):
        weights = jnp.where(lane // slots == e, gates[:, e : e + 1], weights)
    weights = jnp.where(one_hot(ids, local_tokens), weights, 0.0)
    high = weights.astype(jnp.bfloat16)
    low = (weights - high.astype(jnp.float32)).astype(jnp.bfloat16)
    out_ref[...] = jnp.concatenate([high, low], axis=1)


def mix_kernel(core_ref, arrived_ref, weights_ref, out_hbm, out_ref, sems):
    slots, quarter = arrived_ref.shape[1:]
    experts = arrived_ref.shape[0] // (SIDE * SIDE)
    weights = weights_ref[...]
    core = core_ref[0]
    stores = []
    for q in range(QUARTERS):
        total = []
        for e in range(experts):
            part = jnp.zeros((slots, quarter), jnp.float32)
            for a in range(SIDE):
                b = (q - 2 * a) % QUARTERS
                at = jnp.where(core == 0, a * SIDE + b, b * SIDE + a)
                part += arrived_ref[e * SIDE * SIDE + at].astype(jnp.float32)
            total.append(part)
        total = jnp.concatenate(total + total, axis=0).astype(jnp.bfloat16)
        mixed = jnp.dot(weights, total, preferred_element_type=jnp.float32)
        at = pl.ds(q * quarter, quarter)
        out_ref[:, at] = mixed.astype(jnp.bfloat16)
        stores.append(pltpu.make_async_copy(out_ref.at[:, at], out_hbm.at[:, at], sems.at[q]))
        stores[-1].start()
    for store in stores:
        store.wait()


def call(kernel, scalars, arrays, outs, scratch=(), space=pltpu.VMEM):
    vmem = lambda: pl.BlockSpec(memory_space=pltpu.VMEM)
    return pl.pallas_call(
        kernel,
        out_shape=outs,
        in_specs=[pl.BlockSpec(memory_space=pltpu.SMEM) for _ in scalars]
        + [vmem() for _ in arrays],
        out_specs=jax.tree.map(lambda _: pl.BlockSpec(memory_space=space), outs),
        scratch_shapes=list(scratch),
        compiler_params=pltpu.CompilerParams(vmem_limit_bytes=VMEM),
    )(*scalars, *arrays)


def on_device(tokens, router, up_weight, down_weight, choices):
    n_expert = lax.axis_size("expert")
    n_row = lax.axis_size("row")
    sources = n_expert * n_row
    slots = choices.shape[2]
    local_tokens, width = tokens.shape
    quarter = width // QUARTERS
    capacity = PER_SRC * sources
    swap = [(0, 1), (1, 0)]
    core = lax.axis_index("col")
    row = lax.axis_index("row")
    z, y = row // SIDE, row % SIDE
    mine = jnp.where(core == 0, y + 2 * z, z + 2 * y) % QUARTERS
    core_at = core.astype(jnp.int32).reshape(1)
    up_local = up_weight[0]
    down_local = down_weight[0]

    mine_at = mine.astype(jnp.int32).reshape(1)
    place = [mine_at, core_at]
    hidden_units = up_local.shape[1]

    def shape(*dims, dtype=jnp.bfloat16):
        return jax.ShapeDtypeStruct(dims, dtype)

    def send(array, move):
        return lax.ppermute(array, ("row", "col"), pairs_of(move))

    token_rows = jnp.arange(local_tokens, dtype=jnp.int32)
    hot = (choices[0][:, :, None] == token_rows).astype(jnp.bfloat16)
    hot = hot.reshape(n_expert * slots, local_tokens)
    picked = jnp.dot(hot, tokens, preferred_element_type=jnp.float32)
    spread = call(spread_kernel, [core_at], [picked, hot], shape(sources, slots, quarter))
    own = lax.all_to_all(spread, ("expert", "row"), split_axis=0, concat_axis=0, tiled=True)
    full, where = call(
        compact_kernel,
        [],
        [own.reshape(sources * slots, quarter)],
        (shape(capacity, quarter), shape(capacity, 2 * BAND)),
    )
    pieces = [send(full, move) for move in DISPATCH]

    sums = shape(capacity, hidden_units, dtype=jnp.float32)
    up_part = call(first_up_kernel, place, [full, up_local], sums)
    for move, piece in zip(DISPATCH[:-1], pieces):
        kernel = functools.partial(next_up_kernel, move)
        up_part = call(kernel, place, [up_part, piece, up_local], sums)
    up_part, rounded = call(
        functools.partial(last_up_kernel, DISPATCH[-1]),
        place,
        [up_part, pieces[-1], up_local],
        (sums, shape(capacity, hidden_units)),
    )
    other = lax.ppermute(rounded, "col", swap)

    hidden, *pieces = call(
        down_kernel,
        place,
        [up_part, other, down_local],
        (shape(capacity, hidden_units),)
        + tuple(shape(capacity, quarter // 8 * (last - first)) for _, _, first, last in RETURN),
    )
    pieces = [send(piece, move) for piece, move in zip(pieces, RETURN)]
    own, turned = call(
        own_down_kernel,
        [mine_at],
        [hidden, down_local, where],
        (
            shape(capacity, quarter, dtype=jnp.float32),
            shape(sources * slots, 2 * BAND),
        ),
    )
    late_router, own = lax.optimization_barrier((router, own))
    logits = jnp.dot(tokens, late_router, preferred_element_type=jnp.float32)
    weights = call(
        weight_kernel,
        [],
        [choices, logits, lax.ppermute(logits, "col", swap)],
        shape(local_tokens, 2 * n_expert * slots),
    )
    own, weights = lax.optimization_barrier((own, weights))
    out = call(
        return_kernel,
        [],
        [own, *pieces, turned],
        shape(sources * slots, quarter),
    )
    arrived = lax.all_to_all(
        out.reshape(sources, slots, quarter), ("expert", "row"), split_axis=0, concat_axis=0, tiled=True
    )
    return call(
        mix_kernel,
        [core_at],
        [arrived, weights],
        shape(local_tokens, width),
        scratch=[pltpu.VMEM(tokens.shape, jnp.bfloat16), pltpu.SemaphoreType.DMA((QUARTERS,))],
        space=pl.ANY,
    )


def solution(mesh):
    return jax.shard_map(
        on_device,
        mesh=mesh,
        in_specs=(
            P(("expert", "row"), "col"),
            P("col", None),
            P("expert", "col", "row"),
            P("expert", "row", "col"),
            P(("expert", "row"), None, None),
        ),
        out_specs=P(("expert", "row"), "col"),
        check_vma=False,
    )
```

```python
import functools

import jax
import jax.numpy as jnp
from jax import lax
from jax.experimental import pallas as pl
from jax.experimental.pallas import tpu as pltpu
from jax.sharding import PartitionSpec as P

SIDE = 4
QUARTERS = 4
BAND = 128
PER_SRC = 6
EMPTY = 8.0
VMEM = 16 * 1024 * 1024
A, B, LEFT, RIGHT = ("own", 1), ("own", 3), ("other", 1), ("other", 3)
CHANGE = {A: 1, B: 3, LEFT: 2, RIGHT: 2}
DISPATCH = ((B, LEFT, 0, 8), (A, A, 0, 8), (LEFT, B, 0, 8))
RETURN = DISPATCH


def pairs_of(move):
    pairs = []
    for z in range(SIDE):
        for y in range(SIDE):
            for core in range(2):
                axis, flip = move[core]
                along_y = (axis == "own") == (core == 0)
                to = (z * SIDE + (y ^ flip)) if along_y else ((z ^ flip) * SIDE + y)
                pairs.append(((z * SIDE + y) * 2 + core, to * 2 + core))
    return pairs


def class_of(mine_ref, core_ref, move):
    change = [CHANGE[kind] for kind in move[:2]]
    if change[0] == change[1]:
        return mine_ref[0] ^ change[0]
    return mine_ref[0] ^ jnp.where(core_ref[0] == 0, change[0], change[1])


def slot_row(choices):
    experts, slots = choices.shape
    lane = lax.broadcasted_iota(jnp.int32, (slots, experts * slots), 1)
    slot = lax.broadcasted_iota(jnp.int32, (slots, experts * slots), 0)
    tile = (lane % slots == slot).astype(jnp.float32)
    spread = jnp.dot(choices.astype(jnp.float32), tile, preferred_element_type=jnp.float32)
    lane = lax.broadcasted_iota(jnp.int32, spread.shape, 1)
    expert = lax.broadcasted_iota(jnp.int32, spread.shape, 0)
    row = jnp.sum(jnp.where(lane // slots == expert, spread, 0.0), axis=0, keepdims=True)
    return row.astype(jnp.int32)


def one_hot(ids, local_tokens):
    return lax.broadcasted_iota(jnp.int32, (local_tokens, ids.shape[1]), 0) == ids


def spread_kernel(core_ref, picked_ref, hot_ref, out_ref):
    slots, quarter = out_ref.shape[1:]
    experts = out_ref.shape[0] // (SIDE * SIDE)
    live = jnp.sum(hot_ref[...].astype(jnp.float32), axis=1, keepdims=True)
    mark = jnp.broadcast_to((1.0 - live) * EMPTY, (experts * slots, 128))
    core = core_ref[0]
    parts = []
    for q in range(QUARTERS):
        part = picked_ref[:, q * quarter : (q + 1) * quarter]
        part = jnp.concatenate([part[:, :128] + mark, part[:, 128:]], axis=1)
        parts.append(part.reshape(experts, slots, quarter).astype(jnp.bfloat16))
    for a in range(SIDE):
        for b in range(SIDE):
            k0, k1 = (b + 2 * a) % QUARTERS, (a + 2 * b) % QUARTERS
            value = parts[k0] if k0 == k1 else jnp.where(core == 0, parts[k0], parts[k1])
            for e in range(experts):
                out_ref[e * SIDE * SIDE + a * SIDE + b] = value[e]


def compact_kernel(x_ref, full_ref, where_ref):
    rows = x_ref.shape[0]
    capacity = full_ref.shape[0]
    live = (x_ref[:, :128].astype(jnp.float32) < EMPTY - 1.0).astype(jnp.float32)
    i = lax.broadcasted_iota(jnp.int32, (BAND, BAND), 0)
    j = lax.broadcasted_iota(jnp.int32, (BAND, BAND), 1)
    masks = jnp.concatenate([(i < j).astype(jnp.bfloat16), (i == j).astype(jnp.bfloat16)], axis=1)
    offset, position = 0.0, []
    for row in range(0, rows, BAND):
        part = live[row : row + BAND]
        both = lax.dot_general(
            part.astype(jnp.bfloat16), masks, (((0,), (0,)), ((), ())), preferred_element_type=jnp.float32
        )[:8]
        position.append(jnp.where(both[:, BAND:] > 0.5, both[:, :BAND] + offset, -1.0))
        offset += jnp.sum(part, axis=0, keepdims=True)
    position = jnp.concatenate(position, axis=1).astype(jnp.int32)[:1]
    for p in range(0, capacity, BAND):
        columns = slice(p, p + 2 * BAND)
        target = lax.broadcasted_iota(jnp.int32, (BAND, 2 * BAND), 0) + p
        where = (target == position[:, columns]).astype(jnp.bfloat16)
        where_ref[p : p + BAND, :] = where
        full_ref[p : p + BAND, :] = jnp.dot(
            where, x_ref[columns, :], preferred_element_type=jnp.float32
        ).astype(jnp.bfloat16)


def up_product(where, rows_ref, up_ref):
    quarter = rows_ref.shape[1]
    start = pl.multiple_of(where * quarter, quarter)
    return jnp.dot(
        rows_ref[...], up_ref[pl.ds(start, quarter), :], preferred_element_type=jnp.float32
    )


def first_up_kernel(mine_ref, core_ref, rows_ref, up_ref, out_ref):
    out_ref[...] = up_product(mine_ref[0], rows_ref, up_ref)


def next_up_kernel(move, mine_ref, core_ref, sum_ref, rows_ref, up_ref, out_ref):
    at = class_of(mine_ref, core_ref, move)
    out_ref[...] = sum_ref[...] + up_product(at, rows_ref, up_ref)


def last_up_kernel(move, mine_ref, core_ref, sum_ref, rows_ref, up_ref, out_ref, send_ref):
    at = class_of(mine_ref, core_ref, move)
    total = sum_ref[...] + up_product(at, rows_ref, up_ref)
    out_ref[...] = total
    send_ref[...] = total.astype(jnp.bfloat16)


def down_kernel(mine_ref, core_ref, sum_ref, other_ref, down_ref, hidden_ref, *out_refs):
    rows = hidden_ref.shape[0]
    block = rows // 2
    for i in range(2):
        at = slice(i * block, (i + 1) * block)
        value = sum_ref[at, :] + other_ref[at, :].astype(jnp.float32)
        hidden = jax.nn.gelu(value, approximate=True).astype(jnp.bfloat16)
        hidden_ref[at, :] = hidden
        for move, out_ref in zip(RETURN, out_refs):
            first, last = move[2:]
            eighth = out_ref.shape[1] // (last - first)
            start = (class_of(mine_ref, core_ref, move) * 8 + first) * eighth
            columns = pl.ds(pl.multiple_of(start, 2 * eighth), out_ref.shape[1])
            out_ref[at, :] = jnp.dot(
                hidden, down_ref[:, columns], preferred_element_type=jnp.float32
            ).astype(jnp.bfloat16)


def own_down_kernel(mine_ref, hidden_ref, down_ref, where_ref, out_ref, turned_ref):
    quarter = out_ref.shape[1]
    start = pl.multiple_of(mine_ref[0] * quarter, quarter)
    out_ref[...] = jnp.dot(
        hidden_ref[...], down_ref[:, pl.ds(start, quarter)], preferred_element_type=jnp.float32
    )
    for p in range(0, where_ref.shape[0], BAND):
        where = where_ref[p : p + BAND, :].astype(jnp.float32)
        turned_ref[p : p + BAND, BAND:] = where[:, :BAND].T.astype(jnp.bfloat16)
        turned_ref[p + BAND : p + 2 * BAND, :BAND] = where[:, BAND:].T.astype(jnp.bfloat16)


def return_kernel(own_ref, *refs):
    *piece_refs, turned_ref, out_ref = refs
    total = own_ref[...]
    for piece_ref in piece_refs:
        total += piece_ref[...].astype(jnp.float32)
    total = total.astype(jnp.bfloat16)
    for row in range(0, out_ref.shape[0], BAND):
        low, high = max(row - BAND, 0), min(row + BAND, total.shape[0])
        columns = slice(low - row + BAND, high - row + BAND)
        out_ref[row : row + BAND, :] = jnp.dot(
            turned_ref[row : row + BAND, columns], total[low:high], preferred_element_type=jnp.float32
        ).astype(jnp.bfloat16)


def weight_kernel(choices_ref, logits_ref, other_ref, out_ref):
    experts, slots = choices_ref.shape[1:]
    local_tokens = logits_ref.shape[0]
    ids = slot_row(choices_ref[0])
    gates = jax.nn.sigmoid(logits_ref[...] + other_ref[...])
    lane = lax.broadcasted_iota(jnp.int32, (local_tokens, experts * slots), 1)
    weights = jnp.zeros((local_tokens, experts * slots), jnp.float32)
    for e in range(experts):
        weights = jnp.where(lane // slots == e, gates[:, e : e + 1], weights)
    weights = jnp.where(one_hot(ids, local_tokens), weights, 0.0)
    high = weights.astype(jnp.bfloat16)
    low = (weights - high.astype(jnp.float32)).astype(jnp.bfloat16)
    out_ref[...] = jnp.concatenate([high, low], axis=1)


def mix_kernel(core_ref, arrived_ref, weights_ref, out_hbm, out_ref, sems):
    slots, quarter = arrived_ref.shape[1:]
    experts = arrived_ref.shape[0] // (SIDE * SIDE)
    weights = weights_ref[...]
    core = core_ref[0]
    stores = []
    for q in range(QUARTERS):
        total = []
        for e in range(experts):
            part = jnp.zeros((slots, quarter), jnp.float32)
            for a in range(SIDE):
                b = (q - 2 * a) % QUARTERS
                at = jnp.where(core == 0, a * SIDE + b, b * SIDE + a)
                part += arrived_ref[e * SIDE * SIDE + at].astype(jnp.float32)
            total.append(part)
        total = jnp.concatenate(total + total, axis=0).astype(jnp.bfloat16)
        mixed = jnp.dot(weights, total, preferred_element_type=jnp.float32)
        at = pl.ds(q * quarter, quarter)
        out_ref[:, at] = mixed.astype(jnp.bfloat16)
        stores.append(pltpu.make_async_copy(out_ref.at[:, at], out_hbm.at[:, at], sems.at[q]))
        stores[-1].start()
    for store in stores:
        store.wait()


def call(kernel, scalars, arrays, outs, scratch=(), space=pltpu.VMEM):
    vmem = lambda: pl.BlockSpec(memory_space=pltpu.VMEM)
    return pl.pallas_call(
        kernel,
        out_shape=outs,
        in_specs=[pl.BlockSpec(memory_space=pltpu.SMEM) for _ in scalars]
        + [vmem() for _ in arrays],
        out_specs=jax.tree.map(lambda _: pl.BlockSpec(memory_space=space), outs),
        scratch_shapes=list(scratch),
        compiler_params=pltpu.CompilerParams(vmem_limit_bytes=VMEM),
    )(*scalars, *arrays)


def on_device(tokens, router, up_weight, down_weight, choices):
    n_expert = lax.axis_size("expert")
    n_row = lax.axis_size("row")
    sources = n_expert * n_row
    slots = choices.shape[2]
    local_tokens, width = tokens.shape
    quarter = width // QUARTERS
    capacity = PER_SRC * sources
    swap = [(0, 1), (1, 0)]
    core = lax.axis_index("col")
    row = lax.axis_index("row")
    z, y = row // SIDE, row % SIDE
    mine = jnp.where(core == 0, y + 2 * z, z + 2 * y) % QUARTERS
    core_at = core.astype(jnp.int32).reshape(1)
    up_local = up_weight[0]
    down_local = down_weight[0]

    mine_at = mine.astype(jnp.int32).reshape(1)
    place = [mine_at, core_at]
    hidden_units = up_local.shape[1]

    def shape(*dims, dtype=jnp.bfloat16):
        return jax.ShapeDtypeStruct(dims, dtype)

    def send(array, move):
        return lax.ppermute(array, ("row", "col"), pairs_of(move))

    token_rows = jnp.arange(local_tokens, dtype=jnp.int32)
    hot = (choices[0][:, :, None] == token_rows).astype(jnp.bfloat16)
    hot = hot.reshape(n_expert * slots, local_tokens)
    picked = jnp.dot(hot, tokens, preferred_element_type=jnp.float32)
    spread = call(spread_kernel, [core_at], [picked, hot], shape(sources, slots, quarter))
    own = lax.all_to_all(spread, ("expert", "row"), split_axis=0, concat_axis=0, tiled=True)
    full, where = call(
        compact_kernel,
        [],
        [own.reshape(sources * slots, quarter)],
        (shape(capacity, quarter), shape(capacity, 2 * BAND)),
    )
    pieces = [send(full, move) for move in DISPATCH]

    sums = shape(capacity, hidden_units, dtype=jnp.float32)
    up_part = call(first_up_kernel, place, [full, up_local], sums)
    for move, piece in zip(DISPATCH[:-1], pieces):
        kernel = functools.partial(next_up_kernel, move)
        up_part = call(kernel, place, [up_part, piece, up_local], sums)
    up_part, rounded = call(
        functools.partial(last_up_kernel, DISPATCH[-1]),
        place,
        [up_part, pieces[-1], up_local],
        (sums, shape(capacity, hidden_units)),
    )
    other = lax.ppermute(rounded, "col", swap)

    hidden, *pieces = call(
        down_kernel,
        place,
        [up_part, other, down_local],
        (shape(capacity, hidden_units),)
        + tuple(shape(capacity, quarter // 8 * (last - first)) for _, _, first, last in RETURN),
    )
    pieces = [send(piece, move) for piece, move in zip(pieces, RETURN)]
    own, turned = call(
        own_down_kernel,
        [mine_at],
        [hidden, down_local, where],
        (
            shape(capacity, quarter, dtype=jnp.float32),
            shape(sources * slots, 2 * BAND),
        ),
    )
    late_router, own = lax.optimization_barrier((router, own))
    logits = jnp.dot(tokens, late_router, preferred_element_type=jnp.float32)
    weights = call(
        weight_kernel,
        [],
        [choices, logits, lax.ppermute(logits, "col", swap)],
        shape(local_tokens, 2 * n_expert * slots),
    )
    own, weights = lax.optimization_barrier((own, weights))
    out = call(
        return_kernel,
        [],
        [own, *pieces, turned],
        shape(sources * slots, quarter),
    )
    arrived = lax.all_to_all(
        out.reshape(sources, slots, quarter), ("expert", "row"), split_axis=0, concat_axis=0, tiled=True
    )
    return call(
        mix_kernel,
        [core_at],
        [arrived, weights],
        shape(local_tokens, width),
        scratch=[pltpu.VMEM(tokens.shape, jnp.bfloat16), pltpu.SemaphoreType.DMA((QUARTERS,))],
        space=pl.ANY,
    )


def solution(mesh):
    return jax.shard_map(
        on_device,
        mesh=mesh,
        in_specs=(
            P(("expert", "row"), "col"),
            P("col", None),
            P("expert", "col", "row"),
            P("expert", "row", "col"),
            P(("expert", "row"), None, None),
        ),
        out_specs=P(("expert", "row"), "col"),
        check_vma=False,
    )
```

```python
import functools

import jax
import jax.numpy as jnp
from jax import lax
from jax.experimental import pallas as pl
from jax.experimental.pallas import tpu as pltpu
from jax.sharding import PartitionSpec as P

SIDE = 4
QUARTERS = 4
BAND = 128
PER_SRC = 6
EMPTY = 8.0
VMEM = 16 * 1024 * 1024
A, B, LEFT, RIGHT = ("own", 1), ("own", 3), ("other", 1), ("other", 3)
CHANGE = {A: 1, B: 3, LEFT: 2, RIGHT: 2}
DISPATCH = ((B, LEFT, 0, 8), (A, A, 0, 8), (LEFT, B, 0, 8))
RETURN = DISPATCH


def pairs_of(move):
    pairs = []
    for z in range(SIDE):
        for y in range(SIDE):
            for core in range(2):
                axis, flip = move[core]
                along_y = (axis == "own") == (core == 0)
                to = (z * SIDE + (y ^ flip)) if along_y else ((z ^ flip) * SIDE + y)
                pairs.append(((z * SIDE + y) * 2 + core, to * 2 + core))
    return pairs


def class_of(mine_ref, core_ref, move):
    change = [CHANGE[kind] for kind in move[:2]]
    if change[0] == change[1]:
        return mine_ref[0] ^ change[0]
    return mine_ref[0] ^ jnp.where(core_ref[0] == 0, change[0], change[1])


def slot_row(choices):
    experts, slots = choices.shape
    lane = lax.broadcasted_iota(jnp.int32, (slots, experts * slots), 1)
    slot = lax.broadcasted_iota(jnp.int32, (slots, experts * slots), 0)
    tile = (lane % slots == slot).astype(jnp.float32)
    spread = jnp.dot(choices.astype(jnp.float32), tile, preferred_element_type=jnp.float32)
    lane = lax.broadcasted_iota(jnp.int32, spread.shape, 1)
    expert = lax.broadcasted_iota(jnp.int32, spread.shape, 0)
    row = jnp.sum(jnp.where(lane // slots == expert, spread, 0.0), axis=0, keepdims=True)
    return row.astype(jnp.int32)


def one_hot(ids, local_tokens):
    return lax.broadcasted_iota(jnp.int32, (local_tokens, ids.shape[1]), 0) == ids


def spread_kernel(core_ref, picked_ref, hot_ref, out_ref):
    slots, quarter = out_ref.shape[1:]
    experts = out_ref.shape[0] // (SIDE * SIDE)
    live = lax.dot_general(
        hot_ref[...],
        jnp.ones((hot_ref.shape[0], 128), jnp.bfloat16),
        (((0,), (0,)), ((), ())),
        preferred_element_type=jnp.float32,
    )
    mark = (1.0 - live) * EMPTY
    core = core_ref[0]
    parts = []
    for q in range(QUARTERS):
        part = picked_ref[:, q * quarter : (q + 1) * quarter]
        part = jnp.concatenate([part[:, :128] + mark, part[:, 128:]], axis=1)
        parts.append(part.reshape(experts, slots, quarter).astype(jnp.bfloat16))
    for a in range(SIDE):
        for b in range(SIDE):
            k0, k1 = (b + 2 * a) % QUARTERS, (a + 2 * b) % QUARTERS
            value = parts[k0] if k0 == k1 else jnp.where(core == 0, parts[k0], parts[k1])
            for e in range(experts):
                out_ref[e * SIDE * SIDE + a * SIDE + b] = value[e]


def compact_kernel(x_ref, full_ref, where_ref):
    rows = x_ref.shape[0]
    capacity = full_ref.shape[0]
    live = (x_ref[:, :128].astype(jnp.float32) < EMPTY - 1.0).astype(jnp.float32)
    i = lax.broadcasted_iota(jnp.int32, (BAND, BAND), 0)
    j = lax.broadcasted_iota(jnp.int32, (BAND, BAND), 1)
    masks = jnp.concatenate([(i < j).astype(jnp.bfloat16), (i == j).astype(jnp.bfloat16)], axis=1)
    offset, position = 0.0, []
    for row in range(0, rows, BAND):
        part = live[row : row + BAND]
        both = lax.dot_general(
            part.astype(jnp.bfloat16), masks, (((0,), (0,)), ((), ())), preferred_element_type=jnp.float32
        )[:8]
        position.append(jnp.where(both[:, BAND:] > 0.5, both[:, :BAND] + offset, -1.0))
        offset += jnp.sum(part, axis=0, keepdims=True)
    position = jnp.concatenate(position, axis=1).astype(jnp.int32)[:1]
    for p in range(0, capacity, BAND):
        columns = slice(p, p + 2 * BAND)
        target = lax.broadcasted_iota(jnp.int32, (BAND, 2 * BAND), 0) + p
        where = (target == position[:, columns]).astype(jnp.bfloat16)
        where_ref[p : p + BAND, :] = where
        full_ref[p : p + BAND, :] = jnp.dot(
            where, x_ref[columns, :], preferred_element_type=jnp.float32
        ).astype(jnp.bfloat16)


def up_product(where, rows_ref, up_ref):
    quarter = rows_ref.shape[1]
    start = pl.multiple_of(where * quarter, quarter)
    return jnp.dot(
        rows_ref[...], up_ref[pl.ds(start, quarter), :], preferred_element_type=jnp.float32
    )


def first_up_kernel(mine_ref, core_ref, rows_ref, up_ref, out_ref):
    out_ref[...] = up_product(mine_ref[0], rows_ref, up_ref)


def next_up_kernel(move, mine_ref, core_ref, sum_ref, rows_ref, up_ref, out_ref):
    at = class_of(mine_ref, core_ref, move)
    out_ref[...] = sum_ref[...] + up_product(at, rows_ref, up_ref)


def last_up_kernel(move, mine_ref, core_ref, sum_ref, rows_ref, up_ref, out_ref, send_ref):
    at = class_of(mine_ref, core_ref, move)
    total = sum_ref[...] + up_product(at, rows_ref, up_ref)
    out_ref[...] = total
    send_ref[...] = total.astype(jnp.bfloat16)


def down_kernel(mine_ref, core_ref, sum_ref, other_ref, down_ref, hidden_ref, *out_refs):
    rows = hidden_ref.shape[0]
    block = rows // 2
    for i in range(2):
        at = slice(i * block, (i + 1) * block)
        value = sum_ref[at, :] + other_ref[at, :].astype(jnp.float32)
        hidden = jax.nn.gelu(value, approximate=True).astype(jnp.bfloat16)
        hidden_ref[at, :] = hidden
        for move, out_ref in zip(RETURN, out_refs):
            first, last = move[2:]
            eighth = out_ref.shape[1] // (last - first)
            start = (class_of(mine_ref, core_ref, move) * 8 + first) * eighth
            columns = pl.ds(pl.multiple_of(start, 2 * eighth), out_ref.shape[1])
            out_ref[at, :] = jnp.dot(
                hidden, down_ref[:, columns], preferred_element_type=jnp.float32
            ).astype(jnp.bfloat16)


def own_down_kernel(mine_ref, hidden_ref, down_ref, where_ref, out_ref, turned_ref):
    quarter = out_ref.shape[1]
    start = pl.multiple_of(mine_ref[0] * quarter, quarter)
    out_ref[...] = jnp.dot(
        hidden_ref[...], down_ref[:, pl.ds(start, quarter)], preferred_element_type=jnp.float32
    )
    for p in range(0, where_ref.shape[0], BAND):
        where = where_ref[p : p + BAND, :].astype(jnp.float32)
        turned_ref[p : p + BAND, BAND:] = where[:, :BAND].T.astype(jnp.bfloat16)
        turned_ref[p + BAND : p + 2 * BAND, :BAND] = where[:, BAND:].T.astype(jnp.bfloat16)


def return_kernel(own_ref, *refs):
    *piece_refs, turned_ref, out_ref = refs
    total = own_ref[...]
    for piece_ref in piece_refs:
        total += piece_ref[...].astype(jnp.float32)
    total = total.astype(jnp.bfloat16)
    for row in range(0, out_ref.shape[0], BAND):
        low, high = max(row - BAND, 0), min(row + BAND, total.shape[0])
        columns = slice(low - row + BAND, high - row + BAND)
        out_ref[row : row + BAND, :] = jnp.dot(
            turned_ref[row : row + BAND, columns], total[low:high], preferred_element_type=jnp.float32
        ).astype(jnp.bfloat16)


def weight_kernel(choices_ref, logits_ref, other_ref, out_ref):
    experts, slots = choices_ref.shape[1:]
    local_tokens = logits_ref.shape[0]
    ids = slot_row(choices_ref[0])
    gates = jax.nn.sigmoid(logits_ref[...] + other_ref[...])
    lane = lax.broadcasted_iota(jnp.int32, (local_tokens, experts * slots), 1)
    weights = jnp.zeros((local_tokens, experts * slots), jnp.float32)
    for e in range(experts):
        weights = jnp.where(lane // slots == e, gates[:, e : e + 1], weights)
    weights = jnp.where(one_hot(ids, local_tokens), weights, 0.0)
    high = weights.astype(jnp.bfloat16)
    low = (weights - high.astype(jnp.float32)).astype(jnp.bfloat16)
    out_ref[...] = jnp.concatenate([high, low], axis=1)


def mix_kernel(core_ref, arrived_ref, weights_ref, out_hbm, out_ref, sems):
    slots, quarter = arrived_ref.shape[1:]
    experts = arrived_ref.shape[0] // (SIDE * SIDE)
    weights = weights_ref[...]
    core = core_ref[0]
    stores = []
    for q in range(QUARTERS):
        total = []
        for e in range(experts):
            part = jnp.zeros((slots, quarter), jnp.float32)
            for a in range(SIDE):
                b = (q - 2 * a) % QUARTERS
                at = jnp.where(core == 0, a * SIDE + b, b * SIDE + a)
                part += arrived_ref[e * SIDE * SIDE + at].astype(jnp.float32)
            total.append(part)
        total = jnp.concatenate(total + total, axis=0).astype(jnp.bfloat16)
        mixed = jnp.dot(weights, total, preferred_element_type=jnp.float32)
        at = pl.ds(q * quarter, quarter)
        out_ref[:, at] = mixed.astype(jnp.bfloat16)
        stores.append(pltpu.make_async_copy(out_ref.at[:, at], out_hbm.at[:, at], sems.at[q]))
        stores[-1].start()
    for store in stores:
        store.wait()


def call(kernel, scalars, arrays, outs, scratch=(), space=pltpu.VMEM):
    vmem = lambda: pl.BlockSpec(memory_space=pltpu.VMEM)
    return pl.pallas_call(
        kernel,
        out_shape=outs,
        in_specs=[pl.BlockSpec(memory_space=pltpu.SMEM) for _ in scalars]
        + [vmem() for _ in arrays],
        out_specs=jax.tree.map(lambda _: pl.BlockSpec(memory_space=space), outs),
        scratch_shapes=list(scratch),
        compiler_params=pltpu.CompilerParams(vmem_limit_bytes=VMEM),
    )(*scalars, *arrays)


def on_device(tokens, router, up_weight, down_weight, choices):
    n_expert = lax.axis_size("expert")
    n_row = lax.axis_size("row")
    sources = n_expert * n_row
    slots = choices.shape[2]
    local_tokens, width = tokens.shape
    quarter = width // QUARTERS
    capacity = PER_SRC * sources
    swap = [(0, 1), (1, 0)]
    core = lax.axis_index("col")
    row = lax.axis_index("row")
    z, y = row // SIDE, row % SIDE
    mine = jnp.where(core == 0, y + 2 * z, z + 2 * y) % QUARTERS
    core_at = core.astype(jnp.int32).reshape(1)
    up_local = up_weight[0]
    down_local = down_weight[0]

    mine_at = mine.astype(jnp.int32).reshape(1)
    place = [mine_at, core_at]
    hidden_units = up_local.shape[1]

    def shape(*dims, dtype=jnp.bfloat16):
        return jax.ShapeDtypeStruct(dims, dtype)

    def send(array, move):
        return lax.ppermute(array, ("row", "col"), pairs_of(move))

    token_rows = jnp.arange(local_tokens, dtype=jnp.int32)
    hot = (choices.reshape(1, n_expert * slots) == token_rows[:, None]).astype(jnp.bfloat16)
    picked = lax.dot_general(
        hot, tokens, (((0,), (0,)), ((), ())), preferred_element_type=jnp.float32
    )
    spread = call(spread_kernel, [core_at], [picked, hot], shape(sources, slots, quarter))
    own = lax.all_to_all(spread, ("expert", "row"), split_axis=0, concat_axis=0, tiled=True)
    full, where = call(
        compact_kernel,
        [],
        [own.reshape(sources * slots, quarter)],
        (shape(capacity, quarter), shape(capacity, 2 * BAND)),
    )
    pieces = [send(full, move) for move in DISPATCH]

    sums = shape(capacity, hidden_units, dtype=jnp.float32)
    up_part = call(first_up_kernel, place, [full, up_local], sums)
    for move, piece in zip(DISPATCH[:-1], pieces):
        kernel = functools.partial(next_up_kernel, move)
        up_part = call(kernel, place, [up_part, piece, up_local], sums)
    up_part, rounded = call(
        functools.partial(last_up_kernel, DISPATCH[-1]),
        place,
        [up_part, pieces[-1], up_local],
        (sums, shape(capacity, hidden_units)),
    )
    other = lax.ppermute(rounded, "col", swap)

    hidden, *pieces = call(
        down_kernel,
        place,
        [up_part, other, down_local],
        (shape(capacity, hidden_units),)
        + tuple(shape(capacity, quarter // 8 * (last - first)) for _, _, first, last in RETURN),
    )
    pieces = [send(piece, move) for piece, move in zip(pieces, RETURN)]
    own, turned = call(
        own_down_kernel,
        [mine_at],
        [hidden, down_local, where],
        (
            shape(capacity, quarter, dtype=jnp.float32),
            shape(sources * slots, 2 * BAND),
        ),
    )
    late_router, own = lax.optimization_barrier((router, own))
    logits = jnp.dot(tokens, late_router, preferred_element_type=jnp.float32)
    weights = call(
        weight_kernel,
        [],
        [choices, logits, lax.ppermute(logits, "col", swap)],
        shape(local_tokens, 2 * n_expert * slots),
    )
    own, weights = lax.optimization_barrier((own, weights))
    out = call(
        return_kernel,
        [],
        [own, *pieces, turned],
        shape(sources * slots, quarter),
    )
    arrived = lax.all_to_all(
        out.reshape(sources, slots, quarter), ("expert", "row"), split_axis=0, concat_axis=0, tiled=True
    )
    return call(
        mix_kernel,
        [core_at],
        [arrived, weights],
        shape(local_tokens, width),
        scratch=[pltpu.VMEM(tokens.shape, jnp.bfloat16), pltpu.SemaphoreType.DMA((QUARTERS,))],
        space=pl.ANY,
    )


def solution(mesh):
    return jax.shard_map(
        on_device,
        mesh=mesh,
        in_specs=(
            P(("expert", "row"), "col"),
            P("col", None),
            P("expert", "col", "row"),
            P("expert", "row", "col"),
            P(("expert", "row"), None, None),
        ),
        out_specs=P(("expert", "row"), "col"),
        check_vma=False,
    )
```

```python
import functools

import jax
import jax.numpy as jnp
from jax import lax
from jax.experimental import pallas as pl
from jax.experimental.pallas import tpu as pltpu
from jax.sharding import PartitionSpec as P

SIDE = 4
QUARTERS = 4
BAND = 128
PER_SRC = 6
EMPTY = 8.0
VMEM = 16 * 1024 * 1024
A, B, LEFT, RIGHT = ("own", 1), ("own", 3), ("other", 1), ("other", 3)
CHANGE = {A: 1, B: 3, LEFT: 2, RIGHT: 2}
DISPATCH = ((B, LEFT, 0, 8), (A, A, 0, 8), (LEFT, B, 0, 8))
RETURN = DISPATCH


def pairs_of(move):
    pairs = []
    for z in range(SIDE):
        for y in range(SIDE):
            for core in range(2):
                axis, flip = move[core]
                along_y = (axis == "own") == (core == 0)
                to = (z * SIDE + (y ^ flip)) if along_y else ((z ^ flip) * SIDE + y)
                pairs.append(((z * SIDE + y) * 2 + core, to * 2 + core))
    return pairs


def class_of(mine_ref, core_ref, move):
    change = [CHANGE[kind] for kind in move[:2]]
    if change[0] == change[1]:
        return mine_ref[0] ^ change[0]
    return mine_ref[0] ^ jnp.where(core_ref[0] == 0, change[0], change[1])


def slot_row(choices):
    experts, slots = choices.shape
    lane = lax.broadcasted_iota(jnp.int32, (slots, experts * slots), 1)
    slot = lax.broadcasted_iota(jnp.int32, (slots, experts * slots), 0)
    tile = (lane % slots == slot).astype(jnp.float32)
    spread = jnp.dot(choices.astype(jnp.float32), tile, preferred_element_type=jnp.float32)
    lane = lax.broadcasted_iota(jnp.int32, spread.shape, 1)
    expert = lax.broadcasted_iota(jnp.int32, spread.shape, 0)
    row = jnp.sum(jnp.where(lane // slots == expert, spread, 0.0), axis=0, keepdims=True)
    return row.astype(jnp.int32)


def one_hot(ids, local_tokens):
    return lax.broadcasted_iota(jnp.int32, (local_tokens, ids.shape[1]), 0) == ids


def spread_kernel(core_ref, picked_ref, hot_ref, out_ref):
    slots, quarter = out_ref.shape[1:]
    experts = out_ref.shape[0] // (SIDE * SIDE)
    live = jnp.sum(hot_ref[...].astype(jnp.float32), axis=1, keepdims=True)
    mark = jnp.broadcast_to((1.0 - live) * EMPTY, (experts * slots, 128))
    core = core_ref[0]
    parts = []
    for q in range(QUARTERS):
        part = picked_ref[:, q * quarter : (q + 1) * quarter]
        part = jnp.concatenate([part[:, :128] + mark, part[:, 128:]], axis=1)
        parts.append(part.reshape(experts, slots, quarter).astype(jnp.bfloat16))
    for a in range(SIDE):
        for b in range(SIDE):
            k0, k1 = (b + 2 * a) % QUARTERS, (a + 2 * b) % QUARTERS
            value = parts[k0] if k0 == k1 else jnp.where(core == 0, parts[k0], parts[k1])
            for e in range(experts):
                out_ref[e * SIDE * SIDE + a * SIDE + b] = value[e]


def compact_kernel(x_ref, full_ref, where_ref):
    rows = x_ref.shape[0]
    capacity = full_ref.shape[0]
    live = (x_ref[:, :128].astype(jnp.float32) < EMPTY - 1.0).astype(jnp.float32)
    i = lax.broadcasted_iota(jnp.int32, (BAND, BAND), 0)
    j = lax.broadcasted_iota(jnp.int32, (BAND, BAND), 1)
    masks = jnp.concatenate([(i < j).astype(jnp.bfloat16), (i == j).astype(jnp.bfloat16)], axis=1)
    offset, position = 0.0, []
    for row in range(0, rows, BAND):
        part = live[row : row + BAND]
        both = lax.dot_general(
            part.astype(jnp.bfloat16), masks, (((0,), (0,)), ((), ())), preferred_element_type=jnp.float32
        )[:8]
        position.append(jnp.where(both[:, BAND:] > 0.5, both[:, :BAND] + offset, -1.0))
        offset += jnp.sum(part, axis=0, keepdims=True)
    position = jnp.concatenate(position, axis=1).astype(jnp.int32)[:1]
    for p in range(0, capacity, BAND):
        columns = slice(p, p + 2 * BAND)
        target = lax.broadcasted_iota(jnp.int32, (BAND, 2 * BAND), 0) + p
        where = (target == position[:, columns]).astype(jnp.bfloat16)
        where_ref[p : p + BAND, :] = where
        full_ref[p : p + BAND, :] = jnp.dot(
            where, x_ref[columns, :], preferred_element_type=jnp.float32
        ).astype(jnp.bfloat16)


def up_product(where, rows_ref, up_ref):
    quarter = rows_ref.shape[1]
    start = pl.multiple_of(where * quarter, quarter)
    return jnp.dot(
        rows_ref[...], up_ref[pl.ds(start, quarter), :], preferred_element_type=jnp.float32
    )


def first_up_kernel(mine_ref, core_ref, rows_ref, up_ref, out_ref):
    out_ref[...] = up_product(mine_ref[0], rows_ref, up_ref)


def next_up_kernel(move, mine_ref, core_ref, sum_ref, rows_ref, up_ref, out_ref):
    at = class_of(mine_ref, core_ref, move)
    out_ref[...] = sum_ref[...] + up_product(at, rows_ref, up_ref)


def last_up_kernel(move, mine_ref, core_ref, sum_ref, rows_ref, up_ref, out_ref, send_ref):
    at = class_of(mine_ref, core_ref, move)
    total = sum_ref[...] + up_product(at, rows_ref, up_ref)
    out_ref[...] = total
    send_ref[...] = total.astype(jnp.bfloat16)


def down_kernel(mine_ref, core_ref, sum_ref, other_ref, down_ref, hidden_ref, *out_refs):
    rows = hidden_ref.shape[0]
    block = rows
    for i in range(1):
        at = slice(i * block, (i + 1) * block)
        value = sum_ref[at, :] + other_ref[at, :].astype(jnp.float32)
        hidden = jax.nn.gelu(value, approximate=True).astype(jnp.bfloat16)
        hidden_ref[at, :] = hidden
        for move, out_ref in zip(RETURN, out_refs):
            first, last = move[2:]
            eighth = out_ref.shape[1] // (last - first)
            start = (class_of(mine_ref, core_ref, move) * 8 + first) * eighth
            columns = pl.ds(pl.multiple_of(start, 2 * eighth), out_ref.shape[1])
            out_ref[at, :] = jnp.dot(
                hidden, down_ref[:, columns], preferred_element_type=jnp.float32
            ).astype(jnp.bfloat16)


def own_down_kernel(mine_ref, hidden_ref, down_ref, where_ref, out_ref, turned_ref):
    quarter = out_ref.shape[1]
    start = pl.multiple_of(mine_ref[0] * quarter, quarter)
    out_ref[...] = jnp.dot(
        hidden_ref[...], down_ref[:, pl.ds(start, quarter)], preferred_element_type=jnp.float32
    )
    for p in range(0, where_ref.shape[0], BAND):
        where = where_ref[p : p + BAND, :].astype(jnp.float32)
        turned_ref[p : p + BAND, BAND:] = where[:, :BAND].T.astype(jnp.bfloat16)
        turned_ref[p + BAND : p + 2 * BAND, :BAND] = where[:, BAND:].T.astype(jnp.bfloat16)


def return_kernel(own_ref, *refs):
    *piece_refs, turned_ref, out_ref = refs
    total = own_ref[...]
    for piece_ref in piece_refs:
        total += piece_ref[...].astype(jnp.float32)
    total = total.astype(jnp.bfloat16)
    for row in range(0, out_ref.shape[0], BAND):
        low, high = max(row - BAND, 0), min(row + BAND, total.shape[0])
        columns = slice(low - row + BAND, high - row + BAND)
        out_ref[row : row + BAND, :] = jnp.dot(
            turned_ref[row : row + BAND, columns], total[low:high], preferred_element_type=jnp.float32
        ).astype(jnp.bfloat16)


def weight_kernel(choices_ref, logits_ref, other_ref, out_ref):
    experts, slots = choices_ref.shape[1:]
    local_tokens = logits_ref.shape[0]
    ids = slot_row(choices_ref[0])
    gates = jax.nn.sigmoid(logits_ref[...] + other_ref[...])
    lane = lax.broadcasted_iota(jnp.int32, (local_tokens, experts * slots), 1)
    weights = jnp.zeros((local_tokens, experts * slots), jnp.float32)
    for e in range(experts):
        weights = jnp.where(lane // slots == e, gates[:, e : e + 1], weights)
    weights = jnp.where(one_hot(ids, local_tokens), weights, 0.0)
    high = weights.astype(jnp.bfloat16)
    low = (weights - high.astype(jnp.float32)).astype(jnp.bfloat16)
    out_ref[...] = jnp.concatenate([high, low], axis=1)


def mix_kernel(core_ref, arrived_ref, weights_ref, out_hbm, out_ref, sems):
    slots, quarter = arrived_ref.shape[1:]
    experts = arrived_ref.shape[0] // (SIDE * SIDE)
    weights = weights_ref[...]
    core = core_ref[0]
    stores = []
    for q in range(QUARTERS):
        total = []
        for e in range(experts):
            part = jnp.zeros((slots, quarter), jnp.float32)
            for a in range(SIDE):
                b = (q - 2 * a) % QUARTERS
                at = jnp.where(core == 0, a * SIDE + b, b * SIDE + a)
                part += arrived_ref[e * SIDE * SIDE + at].astype(jnp.float32)
            total.append(part)
        total = jnp.concatenate(total + total, axis=0).astype(jnp.bfloat16)
        mixed = jnp.dot(weights, total, preferred_element_type=jnp.float32)
        at = pl.ds(q * quarter, quarter)
        out_ref[:, at] = mixed.astype(jnp.bfloat16)
        stores.append(pltpu.make_async_copy(out_ref.at[:, at], out_hbm.at[:, at], sems.at[q]))
        stores[-1].start()
    for store in stores:
        store.wait()


def call(kernel, scalars, arrays, outs, scratch=(), space=pltpu.VMEM):
    vmem = lambda: pl.BlockSpec(memory_space=pltpu.VMEM)
    return pl.pallas_call(
        kernel,
        out_shape=outs,
        in_specs=[pl.BlockSpec(memory_space=pltpu.SMEM) for _ in scalars]
        + [vmem() for _ in arrays],
        out_specs=jax.tree.map(lambda _: pl.BlockSpec(memory_space=space), outs),
        scratch_shapes=list(scratch),
        compiler_params=pltpu.CompilerParams(vmem_limit_bytes=VMEM),
    )(*scalars, *arrays)


def on_device(tokens, router, up_weight, down_weight, choices):
    n_expert = lax.axis_size("expert")
    n_row = lax.axis_size("row")
    sources = n_expert * n_row
    slots = choices.shape[2]
    local_tokens, width = tokens.shape
    quarter = width // QUARTERS
    capacity = PER_SRC * sources
    swap = [(0, 1), (1, 0)]
    core = lax.axis_index("col")
    row = lax.axis_index("row")
    z, y = row // SIDE, row % SIDE
    mine = jnp.where(core == 0, y + 2 * z, z + 2 * y) % QUARTERS
    core_at = core.astype(jnp.int32).reshape(1)
    up_local = up_weight[0]
    down_local = down_weight[0]

    mine_at = mine.astype(jnp.int32).reshape(1)
    place = [mine_at, core_at]
    hidden_units = up_local.shape[1]

    def shape(*dims, dtype=jnp.bfloat16):
        return jax.ShapeDtypeStruct(dims, dtype)

    def send(array, move):
        return lax.ppermute(array, ("row", "col"), pairs_of(move))

    token_rows = jnp.arange(local_tokens, dtype=jnp.int32)
    hot = (choices[0][:, :, None] == token_rows).astype(jnp.bfloat16)
    hot = hot.reshape(n_expert * slots, local_tokens)
    picked = jnp.dot(hot, tokens, preferred_element_type=jnp.float32)
    spread = call(spread_kernel, [core_at], [picked, hot], shape(sources, slots, quarter))
    own = lax.all_to_all(spread, ("expert", "row"), split_axis=0, concat_axis=0, tiled=True)
    full, where = call(
        compact_kernel,
        [],
        [own.reshape(sources * slots, quarter)],
        (shape(capacity, quarter), shape(capacity, 2 * BAND)),
    )
    pieces = [send(full, move) for move in DISPATCH]

    sums = shape(capacity, hidden_units, dtype=jnp.float32)
    up_part = call(first_up_kernel, place, [full, up_local], sums)
    for move, piece in zip(DISPATCH[:-1], pieces):
        kernel = functools.partial(next_up_kernel, move)
        up_part = call(kernel, place, [up_part, piece, up_local], sums)
    up_part, rounded = call(
        functools.partial(last_up_kernel, DISPATCH[-1]),
        place,
        [up_part, pieces[-1], up_local],
        (sums, shape(capacity, hidden_units)),
    )
    other = lax.ppermute(rounded, "col", swap)

    hidden, *pieces = call(
        down_kernel,
        place,
        [up_part, other, down_local],
        (shape(capacity, hidden_units),)
        + tuple(shape(capacity, quarter // 8 * (last - first)) for _, _, first, last in RETURN),
    )
    pieces = [send(piece, move) for piece, move in zip(pieces, RETURN)]
    own, turned = call(
        own_down_kernel,
        [mine_at],
        [hidden, down_local, where],
        (
            shape(capacity, quarter, dtype=jnp.float32),
            shape(sources * slots, 2 * BAND),
        ),
    )
    late_router, own = lax.optimization_barrier((router, own))
    logits = jnp.dot(tokens, late_router, preferred_element_type=jnp.float32)
    weights = call(
        weight_kernel,
        [],
        [choices, logits, lax.ppermute(logits, "col", swap)],
        shape(local_tokens, 2 * n_expert * slots),
    )
    own, weights = lax.optimization_barrier((own, weights))
    out = call(
        return_kernel,
        [],
        [own, *pieces, turned],
        shape(sources * slots, quarter),
    )
    arrived = lax.all_to_all(
        out.reshape(sources, slots, quarter), ("expert", "row"), split_axis=0, concat_axis=0, tiled=True
    )
    return call(
        mix_kernel,
        [core_at],
        [arrived, weights],
        shape(local_tokens, width),
        scratch=[pltpu.VMEM(tokens.shape, jnp.bfloat16), pltpu.SemaphoreType.DMA((QUARTERS,))],
        space=pl.ANY,
    )


def solution(mesh):
    return jax.shard_map(
        on_device,
        mesh=mesh,
        in_specs=(
            P(("expert", "row"), "col"),
            P("col", None),
            P("expert", "col", "row"),
            P("expert", "row", "col"),
            P(("expert", "row"), None, None),
        ),
        out_specs=P(("expert", "row"), "col"),
        check_vma=False,
    )
```
